512 devices in a mesh: section: 4 (over x), ed: 64 (over y, z), tp: 2 (over core).
Axes of the slice: x: 4, y: 8, z: 8, core: 2. Of those that a mesh axis runs over, the one named last changes fastest.
Arguments:
- top_cotangent: bfloat16 [4, 2048, 3072], P(None, 'ed', 'tp'), may hold values from -6 to 6
- layer_inputs: bfloat16 [4, 4, 2048, 3072], P('section', None, 'ed', 'tp'), may hold values from -16 to 16
- router_weight: float32 [4, 3072, 8], P('section'), may hold values from -0.109375 to 0.109375
- expert_ids: int32 [4, 4, 2048, 2], P('section', None, 'ed'), may hold values from 0 to 7, all different within a row; in each aligned block of 32 rows (0 to 31, 32 to 63, ..., all dimensions but the last counted through in order) at most 12 rows name the same one
- expert_outputs: bfloat16 [4, 4, 2048, 2, 3072], P('section', None, 'ed', None, 'tp'), may hold values from -1.5 to 1.5
- hidden: bfloat16 [4, 4, 2048, 2, 8192], P('section', None, 'ed', None, 'tp'), may hold values from -6 to 6
Outputs:
- section_cotangents: bfloat16 [4, 4, 2048, 3072], P('section', None, 'ed', 'tp')
- down_grad: bfloat16 [4, 2, 64, 512, 1536], P('section', 'tp', 'ed')
- router_grad: float32 [4, 2, 1536, 8], P('section', 'tp', 'ed')
The draws below stay inside these ranges and needn't reach their ends.
Inputs may be any that keep to these rules, and one draw needn't show every extreme that they name: `expert_ids`: each token names two different experts. In every layer, micro-batch and index of ed (each aligned block of 32 tokens) no expert is named by more than 12 tokens, a bound that some block reaches.
All inputs are finite; a program needn't handle non-finite values.
Results may differ from the reference program's by a relative error of at most 0.0062.
Values may be sent and summed in bfloat16 or wider, within the bound.
A program may use at most 128 MiB of HBM per device.

```python
import math
import jax
import jax.numpy as jnp
import numpy as np
from jax import lax

D = 3072
FF = 8192
EXPERTS = 8
TOP = 2
MICRO = 4
TOK_DEV = 32
WIN = 4
CAP = 12
TOKENS = 2048
SECTIONS = 4
NF = 8
FBLK = 512
DBLK = 1536
N_ED = 64


def with_spikes(drawn, rng, source, target, parts, factor):
    def block_of(position):
        return (jnp.arange(drawn.shape[position]) // (drawn.shape[position] // parts)).reshape((-1,) + (1,) * (drawn.ndim - 1 - position))

    first = jax.random.permutation(rng, parts)[block_of(target)]
    other_side = (block_of(target) + parts // 2) % parts
    return jnp.where((block_of(source) == first) | (block_of(source) == other_side), factor * drawn, drawn)


def level_of(own_key, extent, cuts, low, high):
    def one(dim, shards_of):
        steps = jax.random.uniform(jax.random.fold_in(jax.random.fold_in(own_key, 6), dim), (shards_of,), jnp.float32, low / len(cuts), high / len(cuts))
        return jnp.repeat(jnp.exp(steps), extent[dim] // shards_of).reshape((-1,) + (1,) * (len(extent) - dim - 1))

    factor_of = one(*cuts[0])
    for cut in cuts[1:]:
        factor_of = factor_of * one(*cut)
    return factor_of


def assign_block(rng, own, number, rows, count, top, limit, lean):
    ranking = jax.random.permutation(rng, count)
    crowded, usual = portions_of(count, rows * top, limit, lean, True), portions_of(count, rows * top, limit, lean, False)
    places = jnp.arange(count)

    def named(lengths, rotation):
        used = int((lengths > 0).sum())
        fixed = max(1, used // 4)
        passed = fixed + (places - fixed + rotation * (used - fixed)) % max(1, count - fixed)
        return jnp.zeros((count,), jnp.int32).at[ranking[jnp.where(places < fixed, places, passed)]].set(jnp.asarray(lengths, jnp.int32))

    lengths = jnp.where(number % 4 == 0, named(crowded, number // 4), named(usual, number - number // 4 - 1))
    mixed = jax.random.permutation(jax.random.fold_in(own, 3), count)
    donor, taker = mixed[0:count // 2 * 2:2], mixed[1:count // 2 * 2:2]
    slack = jnp.minimum(lengths[donor] - 1, limit - lengths[taker]) // 2
    slack = jnp.where((donor == ranking[0]) | (taker == ranking[0]) | (lengths[taker] == 0), 0, jnp.maximum(slack, 0))
    passed = jax.random.randint(jax.random.fold_in(own, 4), (count // 2,), 0, 1 << 20) % (slack + 1)
    lengths = lengths.at[donor].add(-passed).at[taker].add(passed)
    labels = jnp.searchsorted(jnp.cumsum(lengths), jnp.arange(rows * top), side="right").astype(jnp.int32)
    table = labels.reshape(top, rows).T
    table = table[jax.random.permutation(jax.random.fold_in(own, 1), rows)]
    rotation = jax.random.randint(jax.random.fold_in(own, 2), (rows, 1), 0, top)
    return jnp.take_along_axis(table, (jnp.arange(top)[None, :] + rotation) % top, axis=1)


def portions_of(count, total, reach, skew, full):
    portions = [(1 << 20) // math.isqrt(standing ** skew) + 1 for standing in range(1, count + 1)]
    largest = reach if full else min(reach, max(-(-total // count), total * portions[0] // sum(portions)))
    least = 1 if total - largest >= count - 1 else 0
    given, rest = [largest] + [least] * (count - 1), total - largest - least * (count - 1)
    while rest > 0:
        candidates = [i for i in range(1, count) if given[i] < largest] or [i for i in range(1, count) if given[i] < reach]
        pool, left = sum([portions[i] for i in candidates]), rest
        for i in candidates:
            extra = min(reach - given[i], max(1, left * portions[i] // pool), rest)
            given[i] = given[i] + extra
            rest = rest - extra
    return np.array(given)


def noise(rng, dims, deviation, limit, pieces=(), kind=jnp.bfloat16):
    drawn = deviation * jax.random.normal(rng, dims, jnp.float32)
    if pieces:
        drawn = drawn * level_of(rng, dims, pieces, -0.22, 0.18)
    return jnp.clip(drawn, -limit, limit).astype(kind)


def gaussian_with(stream_key, dims, spread, limit, pieces, heavy, kind=jnp.bfloat16):
    entries = spread * jax.random.normal(stream_key, dims, jnp.float32)
    if pieces:
        entries = entries * level_of(stream_key, dims, pieces, -0.22, 0.18)
    return jnp.clip(with_spikes(entries, jax.random.fold_in(stream_key, 3), *heavy), -limit, limit).astype(kind)


def setup_inputs(seed: int = 0) -> dict:
    streams_of = jax.random.split(jax.random.key(seed), 7)
    top_cotangent = noise(streams_of[0], (MICRO, TOKENS, D), 1.0, 6.0, ((1, 64), (2, 2)))
    layer_inputs = gaussian_with(streams_of[1], (SECTIONS, MICRO, TOKENS, D), 1.0, 16.0, ((0, 4), (2, 64), (3, 2)), (2, 3, 64, 4.0))
    router_weight = noise(streams_of[2], (SECTIONS, D, EXPERTS), D ** -0.5, 0.109375, ((0, 4),), jnp.float32)
    expert_ids_keys = jax.random.split(jax.random.fold_in(streams_of[3], 1), SECTIONS * MICRO * TOKENS // TOK_DEV)
    expert_ids_turns = jax.random.permutation(jax.random.fold_in(streams_of[3], 3), SECTIONS * MICRO * TOKENS // TOK_DEV)
    expert_ids = jax.vmap(lambda own, number: assign_block(jax.random.fold_in(streams_of[3], 2), own, number, TOK_DEV, EXPERTS, TOP, CAP, 2))(expert_ids_keys, expert_ids_turns).reshape((SECTIONS, MICRO, TOKENS, TOP))
    expert_outputs = noise(streams_of[4], (SECTIONS, MICRO, TOKENS, TOP, D), 0.25, 1.5, ((0, 4), (2, 64), (4, 2)))
    hidden = noise(streams_of[5], (SECTIONS, MICRO, TOKENS, TOP, FF), 1.0, 6.0, ((0, 4), (2, 64), (4, 2)))
    return {"top_cotangent": top_cotangent, "layer_inputs": layer_inputs, "router_weight": router_weight, "expert_ids": expert_ids, "expert_outputs": expert_outputs, "hidden": hidden}


def expert_grads(hidden_layer, scaled, ids):
    rows = hidden_layer.shape[0] * hidden_layer.shape[1] * hidden_layer.shape[2]
    flat_hidden = hidden_layer.reshape(rows, FF)
    flat_scaled = scaled.reshape(rows, D)
    flat_ids = ids.reshape(rows)
    most = N_ED * MICRO * CAP
    positions = jnp.arange(rows, dtype=jnp.int32)

    def one_expert(expert):
        match = flat_ids == expert
        rank = jnp.cumsum(match.astype(jnp.int32)) - 1
        target = jnp.where(match, rank, most).astype(jnp.int32)
        order = jnp.zeros((most,), jnp.int32).at[target].set(positions, mode="drop")
        count = jnp.sum(match.astype(jnp.int32))
        keep = (jnp.arange(most, dtype=jnp.int32) < count).astype(flat_scaled.dtype)
        picked_hidden = flat_hidden[order]
        picked_scaled = flat_scaled[order] * keep[:, None]
        total = jnp.dot(picked_hidden.T, picked_scaled, preferred_element_type=jnp.float32)
        return total.astype(jnp.bfloat16)

    grads = lax.map(one_expert, jnp.arange(WIN, dtype=jnp.int32))
    grads = grads.reshape(WIN, 2, NF, FBLK, 2, DBLK).transpose(1, 0, 2, 4, 3, 5)
    return grads.reshape(2, WIN * NF * 2, FBLK, DBLK)


def reference(top_cotangent, layer_inputs, router_weight, expert_ids, expert_outputs, hidden):
    sections = layer_inputs.shape[0]
    iota_e = jnp.arange(EXPERTS, dtype=jnp.int32)
    upstream = top_cotangent
    cot_list = [None] * sections
    down_list = [None] * sections
    router_list = [None] * sections
    for layer in range(sections - 1, -1, -1):
        inputs32 = layer_inputs[layer].astype(jnp.float32)
        weights = router_weight[layer]
        ids = expert_ids[layer]
        logits = jnp.einsum("mtd,de->mte", inputs32, weights, precision=lax.Precision.HIGHEST)
        onehot = (ids[..., None] == iota_e).astype(jnp.float32)
        picked = jnp.sum(onehot * logits[:, :, None, :], axis=-1)
        first = 1.0 / (1.0 + jnp.exp(picked[..., 1] - picked[..., 0]))
        gates = jnp.stack([first, 1.0 - first], axis=-1)
        up32 = upstream.astype(jnp.float32)
        gate_grad = jnp.einsum("mtd,mtkd->mtk", up32, expert_outputs[layer].astype(jnp.float32),
                               precision=lax.Precision.HIGHEST)
        logit_grad = first * (1.0 - first) * (gate_grad[..., 0] - gate_grad[..., 1])
        dlogits = logit_grad[..., None] * (onehot[:, :, 0, :] - onehot[:, :, 1, :])
        back = jnp.einsum("mte,de->mtd", dlogits, weights, precision=lax.Precision.HIGHEST)
        cotangent = (up32 + back).astype(jnp.bfloat16)
        router_full = jnp.einsum("mtd,mte->de", inputs32, dlogits, precision=lax.Precision.HIGHEST)
        router_list[layer] = router_full.reshape(2, D // 2, EXPERTS)
        scaled = (gates[..., None] * up32[:, :, None, :]).astype(jnp.bfloat16)
        down_list[layer] = expert_grads(hidden[layer], scaled, ids)
        cot_list[layer] = cotangent
        upstream = cotangent
    return jnp.stack(cot_list), jnp.stack(down_list), jnp.stack(router_list)
```

```python
import jax
import jax.numpy as jnp
from jax import lax
from jax.experimental import pallas as pl
from jax.experimental.pallas import tpu as pltpu
from jax.sharding import PartitionSpec as P

CAP = 12
MICRO = 4
TOK = 32
SIDE = 8
SECTIONS = 4
EXPERTS = 8
WINDOW = 4
HIGHEST = lax.Precision.HIGHEST
F32 = jnp.float32
BF16 = jnp.bfloat16
MESH = pl.DeviceIdType.MESH


def iota(shape, dim):
    return lax.broadcasted_iota(jnp.int32, shape, dim)


def divided(x, by):
    return ((x.astype(F32) + 0.5) * (1.0 / by)).astype(jnp.int32)


def contract(a, b, da, db, precision=None):
    return lax.dot_general(a, b, (((da,), (db,)), ((), ())), precision=precision, preferred_element_type=F32)


def split2(x):
    hi = x.astype(BF16)
    return hi, (x - hi.astype(F32)).astype(BF16)


def split3(x):
    hi = x.astype(BF16)
    rest = x - hi.astype(F32)
    mid = rest.astype(BF16)
    return hi, mid, (rest - mid.astype(F32)).astype(BF16)


def by_parts(x, rows, dims):
    parts = jnp.concatenate([p.astype(F32) for p in split3(x)], axis=0).astype(BF16)
    got = contract(parts, rows, 1, dims)
    n = x.shape[0]
    return got[:n] + got[n:2 * n] + got[2 * n:]


def earlier(segment_log2):
    r, c = iota((256, 256), 0), iota((256, 256), 1)
    same = jnp.right_shift(r, segment_log2) == jnp.right_shift(c, segment_log2)
    return jnp.where(same & (r < c), 1.0, 0.0).astype(BF16)


def kernel(
    top_ref, x_ref, w_ref, idr_ref, idt_ref, eo_ref, hid_ref,
    cot_ref, down_ref, router_ref,
    wb, pr, sm, szr, sg, ry, ryr, rz, rzr, topb, pick, hs, hy, hz, perm, seg, wq, xs, rel, sc, acc,
    w_s, w_r, p_s, p_r, tz_s, tz_r, ring_s, ring_r, sz_s, sz_r, sy_s, sy_r, ry_s, ry_r, rz_s, rz_r,
    hy_s, hy_r, hz_s, hz_r, hf_s, xx_s, xx_r, rr_s, rr_r, cc_s, cc_r,
):
    x = lax.axis_index("section")
    ed = lax.axis_index("ed")
    c = lax.axis_index("tp")
    y = ed // SIDE
    z = ed % SIDE
    half = top_ref.shape[2]
    quarter = half // 2
    own_half = z % 2
    own_expert = y // 2

    def at_x(k):
        return ((x + k) % SECTIONS, ed, c)

    def at_y(k):
        return (x, ((y + k) % SIDE) * SIDE + z, c)

    def at_z(k):
        return (x, y * SIDE + (z + k) % SIDE, c)

    partner = (x, ed, 1 - c)

    def off(i):
        return ((i + 1) // 2) * (1 - 2 * (i % 2))

    def source(i):
        return (y + SIDE + off(i)) % SIDE

    def copy(src, dst, send, recv, device):
        return pltpu.make_async_remote_copy(
            src_ref=src, dst_ref=dst, send_sem=send, recv_sem=recv, device_id=device, device_id_type=MESH
        )

    barrier = pltpu.get_barrier_semaphore()

    def greet(device):
        pl.semaphore_signal(barrier, inc=1, device_id=device, device_id_type=MESH)

    greet(partner)
    for k in range(1, SECTIONS):
        for cc in range(2):
            greet(((x + k) % SECTIONS, ed, cc))
    for k in range(1, SIDE):
        greet(at_y(k))
        for cc in range(2):
            greet((x, y * SIDE + (z + k) % SIDE, cc))

    ids_row = idr_ref[...]
    named = (jnp.broadcast_to(ids_row, (8, 256)) == iota((8, 256), 0)).astype(F32)
    rank = jnp.dot(named.astype(BF16), earlier(6), preferred_element_type=F32)
    r48 = iota((48, 256), 0)
    m48 = divided(r48, CAP)
    s48 = (r48 - CAP * m48).astype(F32)
    own_micro = m48 == jnp.right_shift(iota((48, 256), 1), 6)
    for e in range(WINDOW):
        hit = (
            (jnp.broadcast_to(named[e:e + 1], (48, 256)) > 0.5)
            & (jnp.broadcast_to(rank[e:e + 1], (48, 256)) == s48)
            & own_micro
        )
        pick[e * 48:(e + 1) * 48, :] = jnp.where(hit, 1.0, 0.0).astype(BF16)

    pl.semaphore_wait(barrier, 1 + 2 * (SECTIONS - 1) + 3 * (SIDE - 1))

    def w_copy(k):
        return copy(w_ref, wb.at[x], w_s.at[k - 1], w_r.at[k - 1], at_x(k))

    for k in range(1, SECTIONS):
        w_copy(k).start()
    wb[x] = w_ref[...]

    tilt = (z + c) % 2
    local = tilt == 0

    def tz_copy(r, cc):
        zd = (z + 2 * r + tilt) % SIDE
        return copy(
            top_ref.at[x, :, pl.ds(cc * quarter, quarter)], topb.at[y, z], tz_s.at[r, cc], tz_r.at[z],
            (x, y * SIDE + zd, cc),
        )

    for r in range(4):
        for cc in range(2):
            if r == 0:
                @pl.when(jnp.logical_not(local & (c == cc)))
                def _():
                    tz_copy(r, cc).start()
            else:
                tz_copy(r, cc).start()

    @pl.when(local)
    def _():
        topb[y, z] = top_ref[x, :, pl.ds(pl.multiple_of(c * quarter, 128), quarter)]

    def hidden_block(f, carry):
        cols = hid_ref[:, pl.ds(pl.multiple_of(f * 512, 512), 512)]
        got = jnp.dot(pick[...], cols, preferred_element_type=F32).astype(BF16)
        for e in range(WINDOW):
            hs[2 * e + f // 4, f % 4] = got[e * 48:(e + 1) * 48]
        return carry

    lax.fori_loop(0, 8, hidden_block, 0)

    def hy_copy(i):
        yd = (y + SIDE - off(i)) % SIDE
        return copy(hs.at[yd], hy.at[y], hy_s.at[0], hy_r.at[i], (x, yd * SIDE + z, c))

    def hy_start(i, carry):
        hy_copy(i).start()
        return carry

    def ring_copy(block, first, count, item, k):
        part = topb.at[block, pl.ds(first, count)]
        return copy(part, part, ring_s.at[0], ring_r.at[item], at_y(k))

    def tz_wait(zs, carry):
        @pl.when(jnp.logical_not(local & (zs == z)))
        def _():
            copy(topb.at[y, zs], topb.at[y, zs], tz_s.at[0, 0], tz_r.at[zs], partner).wait_recv()
        return carry

    lax.fori_loop(0, SIDE, tz_wait, 0)
    ring_copy(y, 0, SIDE, 1, 1).start()
    ring_copy(y, 0, SIDE, 2, SIDE - 1).start()
    lax.fori_loop(1, 5, hy_start, 0)
    hy[y] = hs[y]

    pair = z // 2
    parity = z % 2

    def hz_copy(i, d):
        ys = source(i)
        if d == 0:
            target, j = z + 1 - 2 * parity, 1
        elif d == 1:
            target, j = 2 * ((pair + 1) % 4), 0
        elif d == 2:
            target, j = 2 * ((pair + 2) % 4) + 1 - parity, 0
        else:
            target, j = 2 * ((pair + 3) % 4) + 1, 0
        return copy(
            hy.at[ys, (pair + d) % 4], hz.at[z, ys], hz_s.at[0], hz_r.at[i, j], (x, y * SIDE + target, c)
        )

    def send_hidden(i):
        ys = source(i)
        for d in (2, 1, 3, 0):
            hz_copy(i, d).start()
        hz[z, ys] = hy[ys, pair]

    near = 2 * ((pair + 3 + 2 * parity) % 4)
    far = 2 * ((pair + 2) % 4) + 1 - parity
    other = (x, y * SIDE + z + 1 - 2 * parity, c)

    def forward_hidden(i):
        ys = source(i)
        three = hz.at[pl.ds(0, 3), ys]
        copy(three, three, hz_s.at[0], hz_r.at[i, 0], partner).wait_recv()
        two, one = hz.at[pl.ds(near, 2), ys], hz.at[far, ys]
        copy(two, two, hf_s.at[0], hz_r.at[i, 1], other).start()
        copy(one, one, hf_s.at[0], hz_r.at[i, 1], other).start()

    def wait_hidden(i):
        four = hz.at[pl.ds(0, 4), source(i)]
        copy(four, four, hz_s.at[0], hz_r.at[i, 1], partner).wait_recv()

    send_hidden(0)

    core_cols = pl.ds(pl.multiple_of(c * half, 128), half)
    inputs = x_ref[...]
    top_tokens = top_ref[...].reshape(MICRO * TOK, half)
    outs = eo_ref[...]
    r128, c256 = iota((128, 256), 0), iota((128, 256), 1)
    pairs = jnp.where(c256 == 2 * r128, 1.0, jnp.where(c256 == 2 * r128 + 1, -1.0, 0.0))
    pr[x, c, 0:8] = by_parts(w_ref[:, core_cols], inputs, 1)
    products = contract(top_tokens, outs, 1, 1)
    dots = jnp.sum(products * jnp.abs(pairs), axis=0, keepdims=True)
    pr[x, c, 8:16] = contract(jnp.broadcast_to(dots, (8, 256)), pairs, 1, 1, HIGHEST)
    pr[x, c, 9:11] = idt_ref[...]

    def w_wait(k):
        copy(w_ref, wb.at[(x + SECTIONS - k) % SECTIONS], w_s.at[k - 1], w_r.at[k - 1], at_x(k)).wait_recv()

    for k in range(1, SECTIONS):
        w_wait(k)
    weights_half = wb[:, :, core_cols]
    crossed = by_parts(weights_half.reshape(SECTIONS * EXPERTS, half), outs, 1)
    pr[x, c, 16:48] = contract(crossed, pairs, 1, 1, HIGHEST)

    def p_copy(n):
        dx, dc = n // 2, n % 2
        return copy(pr.at[x, c], pr.at[x, c], p_s.at[n - 1], p_r.at[n - 1], ((x + dx) % SECTIONS, ed, (c + dc) % 2))

    for n in range(1, 2 * SECTIONS):
        p_copy(n).start()

    seg[...] = earlier(5)
    rp, cp = iota((384, 384), 0), iota((384, 384), 1)
    qp = divided(rp, CAP)
    perm[...] = jnp.where(
        cp == (qp & 7) * 48 + jnp.right_shift(qp, 3) * CAP + rp - CAP * qp, 1.0, 0.0
    ).astype(BF16)
    w_quarter = wb[:, :, pl.ds(pl.multiple_of(own_half * half + c * quarter, 128), quarter)]
    w_hi, w_mid = split2(w_quarter.reshape(SECTIONS * EXPERTS, quarter))
    wq[0:32] = w_hi
    wq[32:64] = w_hi
    wq[64:96] = w_mid
    wq[96:128] = jnp.zeros((32, quarter), BF16)
    ry[...] = jnp.zeros_like(ry)
    rz[...] = jnp.zeros_like(rz)

    for n in range(1, 2 * SECTIONS):
        dx, dc = n // 2, n % 2
        part = pr.at[(x + SECTIONS - dx) % SECTIONS, (c + dc) % 2]
        copy(part, part, p_s.at[n - 1], p_r.at[n - 1], partner).wait_recv()

    j8 = iota((8, 128), 0).astype(F32)
    firsts, grads, selects, dls = [], [None] * SECTIONS, [], [None] * SECTIONS
    for l in range(SECTIONS):
        logits = pr[l, 0, 0:8] + pr[l, 1, 0:8]
        id0, id1 = pr[l, 0, 9:10], pr[l, 0, 10:11]
        hot0 = jnp.where(jnp.broadcast_to(id0, (8, 128)) == j8, 1.0, 0.0)
        hot1 = jnp.where(jnp.broadcast_to(id1, (8, 128)) == j8, 1.0, 0.0)
        selects.append(hot0 - hot1)
        gap = jnp.sum(hot1 * logits, axis=0, keepdims=True) - jnp.sum(hot0 * logits, axis=0, keepdims=True)
        firsts.append(1.0 / (1.0 + jnp.exp(gap)))
        sm[4 + l:5 + l] = firsts[l]
        sm[8 + l:9 + l] = id0
        sm[12 + l:13 + l] = id1
    for l in range(SECTIONS - 1, -1, -1):
        total = pr[l, 0, 8:9] + pr[l, 1, 8:9]
        for a in range(l + 1, SECTIONS):
            cross = pr[l, 0, 16 + 8 * a:24 + 8 * a] + pr[l, 1, 16 + 8 * a:24 + 8 * a]
            total = total + grads[a] * jnp.sum(cross * selects[a], axis=0, keepdims=True)
        grads[l] = firsts[l] * (1.0 - firsts[l]) * total
        sm[l:l + 1] = grads[l]
        dls[l] = jnp.broadcast_to(grads[l], (8, 128)) * selects[l]

    to = iota((128, 256), 1) - z * TOK
    at = iota((128, 256), 0) - x * TOK
    put = jnp.where((to == at) & (to >= 0) & (to < TOK), 1.0, 0.0)
    szr[z] = jnp.dot(sm[...], put, precision=HIGHEST, preferred_element_type=F32)

    def sz_copy(k):
        return copy(szr.at[z], szr.at[z], sz_s.at[k - 1], sz_r.at[k - 1], at_z(k))

    for k in range(1, SIDE):
        sz_copy(k).start()

    def take_ring(i):
        part = topb.at[source(i)]
        copy(part, part, ring_s.at[0], ring_r.at[i], partner).wait_recv()

        @pl.when(i < 5)
        def _():
            ring_copy(source(i), 0, SIDE, i + 2, 1 + (1 - i % 2) * (SIDE - 2)).start()

        @pl.when(i == 5)
        def _():
            ring_copy(source(i), 0, 4, SIDE - 1, 1).start()

        @pl.when(i == 6)
        def _():
            ring_copy(source(i), 4, 4, SIDE - 1, SIDE - 1).start()

        @pl.when((i >= 2) & (i < 5))
        def _():
            hy_copy(i + 3).start()

    own_dl = jnp.zeros((8, 128), F32)
    for l in range(SECTIONS):
        own_dl = jnp.where(x == l, dls[l], own_dl)
    router_part = by_parts(own_dl, inputs, 0)
    strip = half // SIDE
    for k in range(SIDE):
        ry[k, :, 0:strip] = router_part[:, k * strip:(k + 1) * strip]

    def ry_copy(k):
        yd = (y + k) % SIDE
        return copy(ry.at[yd], ryr.at[y], ry_s.at[k - 1], ry_r.at[k - 1], at_y(k))

    for k in range(1, SIDE):
        ry_copy(k).start()
    ryr[y] = ry[y]

    def first_rings(i, carry):
        take_ring(i)
        return carry

    lax.fori_loop(1, 3, first_rings, 0)

    for k in range(1, SIDE):
        part = szr.at[(z + SIDE - k) % SIDE]
        copy(part, part, sz_s.at[k - 1], sz_r.at[k - 1], partner).wait_recv()
    total = szr[0]
    for k in range(1, SIDE):
        total = total + szr[k]
    sg[y] = total

    def sy_copy(i):
        return copy(sg.at[y], sg.at[y], sy_s.at[i], sy_r.at[i], at_y(SIDE - off(i)))

    for i in range(1, SIDE):
        sy_copy(i).start()

    def rz_copy(k):
        zd = (z + k) % SIDE
        return copy(rz.at[zd], rzr.at[z], rz_s.at[k - 1], rz_r.at[k - 1], at_z(k))

    def router_second():
        for k in range(1, SIDE):
            part = ryr.at[(y + SIDE - k) % SIDE]
            copy(part, part, ry_s.at[k - 1], ry_r.at[k - 1], partner).wait_recv()
        total = ryr[0]
        for k in range(1, SIDE):
            total = total + ryr[k]
        piece = strip // SIDE
        for k in range(SIDE):
            rz[k, :, 0:piece] = total[:, k * piece:(k + 1) * piece]
        for k in range(1, SIDE):
            rz_copy(k).start()
        rzr[z] = rz[z]

    def cotangents():
        cotangent = top_tokens
        for l in range(SECTIONS - 1, -1, -1):
            d_hi, d_mid, _ = split3(dls[l])
            w_hi, w_mid, _ = split3(wb[l, :, core_cols])
            left = jnp.concatenate([d.astype(F32) for d in (d_hi, d_mid, d_hi)], axis=0).astype(BF16)
            right = jnp.concatenate([w.astype(F32) for w in (w_hi, w_hi, w_mid)], axis=0).astype(BF16)
            step = contract(left, right, 0, 0)
            cotangent = jnp.where(l >= x, (cotangent.astype(F32) + step).astype(BF16), cotangent)
        cot_ref[...] = cotangent

    def take_hidden(i):
        copy(hs.at[0], hy.at[source(i)], hy_s.at[0], hy_r.at[i], partner).wait_recv()
        send_hidden(i)

    def x_copy(i, n):
        ys = source(i)
        if n < 2:
            k = 1 + 2 * n
            return copy(
                xs.at[i, (x + k) % SECTIONS], sc.at[c, ys, x], xx_s.at[0], xx_r.at[i], at_x(k)
            )
        n -= 2
        return copy(
            xs.at[i, (x + 2) % SECTIONS, pl.ds(48 * n, 48)], rel.at[i, n], xx_s.at[0], rr_r.at[i, n],
            at_x(1 + 2 * n),
        )

    def relay_copy(i, n):
        k = 1 + 2 * n
        return copy(
            rel.at[i, n], sc.at[c, source(i), (x + SECTIONS - k) % SECTIONS, pl.ds(48 * n, 48)],
            rr_s.at[0], xx_r.at[i], at_x(k),
        )

    def relay(i):
        for n in range(2):
            copy(rel.at[i, n], rel.at[i, n], rr_s.at[0], rr_r.at[i, n], partner).wait_recv()
            relay_copy(i, n).start()

    def core_copy(i):
        part = sc.at[c, source(i)]
        return copy(part, part, cc_s.at[0], cc_r.at[i], partner)

    r96 = iota((96, 256), 0)
    z96 = divided(r96, CAP)
    s96 = (r96 - CAP * z96).astype(F32)
    own_block = z96 == jnp.right_shift(iota((96, 256), 1), 5)
    mine = own_expert.astype(F32)

    def select(i):
        ys = source(i)
        small = sg[ys]
        grad, first, id0, id1 = small[0:4], small[4:8], small[8:12], small[12:16]
        is0, is1 = id0 == mine, id1 == mine
        named = jnp.where(is0 | is1, 1.0, 0.0)
        gate = jnp.where(is0, first, 1.0 - first)
        rank = jnp.dot(
            jnp.concatenate([named, named], axis=0).astype(BF16), seg[...], preferred_element_type=F32
        )
        dl = []
        jt = iota((8, 256), 0).astype(F32)
        for l in range(SECTIONS):
            sel = jnp.where(jnp.broadcast_to(id0[l:l + 1], (8, 256)) == jt, 1.0, 0.0)
            sel = sel - jnp.where(jnp.broadcast_to(id1[l:l + 1], (8, 256)) == jt, 1.0, 0.0)
            dl.append(jnp.broadcast_to(grad[l:l + 1], (8, 256)) * sel)
        d_hi, d_mid = split2(jnp.concatenate(dl, axis=0))
        side = jnp.concatenate([d_hi, d_mid, d_hi, jnp.zeros_like(d_hi)], axis=0)
        tops = topb[ys].reshape(SIDE * TOK, quarter)
        places, gates = [], []
        for l in range(SECTIONS):
            hit = (
                (jnp.broadcast_to(named[l:l + 1], (96, 256)) > 0.5)
                & (jnp.broadcast_to(rank[l:l + 1], (96, 256)) == s96)
                & own_block
            )
            gates.append(jnp.sum(
                jnp.where(hit, jnp.broadcast_to(gate[l:l + 1], (96, 256)), 0.0), axis=1, keepdims=True
            ))
            places.append(jnp.where(hit, 1.0, 0.0).astype(BF16))
        place = jnp.concatenate(places, axis=0)
        lefts = contract(place, side, 1, 1)
        above = jnp.right_shift(iota((96, 128), 1) & 31, 3)
        left = jnp.concatenate(
            [jnp.where(above > l, lefts[96 * l:96 * (l + 1)], 0.0).astype(BF16) for l in range(SECTIONS)], axis=0
        )
        rows = jnp.dot(place, tops, preferred_element_type=F32)
        rows = rows + jnp.dot(left, wq[...], preferred_element_type=F32)
        for l in range(SECTIONS):
            xs[i, l] = (gates[l] * rows[96 * l:96 * (l + 1)]).astype(BF16)
        for n in (2, 3, 0, 1):
            x_copy(i, n).start()
        sc[c, ys, x] = xs[i, x]

    def to_partner(i):
        three = sc.at[c, source(i), pl.ds(0, 3)]
        copy(three, three, xx_s.at[0], xx_r.at[i], partner).wait_recv()
        core_copy(i).start()

    def accumulate(i):
        ys = source(i)
        wait_hidden(i)
        part = sc.at[1 - c, ys]
        copy(part, part, cc_s.at[0], cc_r.at[i], partner).wait_recv()
        rows = jnp.dot(perm[...], hz[:, ys].reshape(384, 512), preferred_element_type=F32).astype(BF16)
        for q in range(2):
            cols = slice(q * quarter, (q + 1) * quarter)
            acc[:, cols] += contract(rows, sc[q, ys].reshape(384, quarter), 0, 0)

    acc[...] = jnp.zeros_like(acc)

    def small_wait(i):
        copy(sg.at[source(i)], sg.at[source(i)], sy_s.at[i], sy_r.at[i], partner).wait_recv()

    def body(i, carry):
        @pl.when((i >= 1) & (i < SIDE - 2))
        def _():
            take_ring(i + 2)

        @pl.when(i < SIDE - 1)
        def _():
            take_hidden(i + 1)

        @pl.when((i >= 1) & (i < SIDE))
        def _():
            small_wait(i)

        @pl.when(i < SIDE)
        def _():
            select(i)

        @pl.when((i >= 1) & (i < SIDE + 1))
        def _():
            forward_hidden(i - 1)
            relay(i - 1)

        @pl.when((i >= 2) & (i < SIDE + 2))
        def _():
            to_partner(i - 2)

        @pl.when(i == 2)
        def _():
            router_second()

        @pl.when(i == 1)
        def _():
            cotangents()

        @pl.when(i >= 3)
        def _():
            accumulate(i - 3)

        return carry

    lax.fori_loop(0, SIDE + 3, body, 0)
    down_ref[...] = acc[...].astype(BF16)
    for k in range(1, SIDE):
        part = rzr.at[(z + SIDE - k) % SIDE]
        copy(part, part, rz_s.at[k - 1], rz_r.at[k - 1], partner).wait_recv()
    total = rzr[0]
    for k in range(1, SIDE):
        total = total + rzr[k]
    router_ref[...] = total

    for k in range(1, SECTIONS):
        w_copy(k).wait_send()
    for n in range(1, 2 * SECTIONS):
        p_copy(n).wait_send()
    for r in range(4):
        for cc in range(2):
            if r == 0:
                @pl.when(jnp.logical_not(local & (c == cc)))
                def _():
                    tz_copy(r, cc).wait_send()
            else:
                tz_copy(r, cc).wait_send()
    for k in range(1, SIDE):
        sz_copy(k).wait_send()
        sy_copy(k).wait_send()
        ry_copy(k).wait_send()
        rz_copy(k).wait_send()


    def drained(ref, sem):
        copy(ref, ref, sem.at[0], cc_r.at[0], partner).wait_send()

    drained(topb.at[pl.ds(0, SIDE - 1)], ring_s)
    drained(hy.at[pl.ds(0, SIDE - 1)], hy_s)
    drained(hy, hz_s)
    drained(hy.at[:, pl.ds(0, 3)], hf_s)
    drained(xs.at[:, pl.ds(0, 3)], xx_s)
    drained(rel, rr_s)
    drained(xs, cc_s)


def per_device(top_cotangent, layer_inputs, router_weight, expert_ids, expert_outputs, hidden):
    micro, tok, half = top_cotangent.shape
    tokens = micro * tok
    half_ff = hidden.shape[4]
    width = router_weight.shape[1]
    quarter = half // 2
    tile = half_ff // SIDE
    strip = half // SIDE // SIDE
    vmem = pl.BlockSpec(memory_space=pltpu.VMEM)
    dma = pltpu.SemaphoreType.DMA
    hidden_rows = MICRO * CAP
    scratch = [
        pltpu.VMEM((SECTIONS, EXPERTS, width), F32),
        pltpu.VMEM((SECTIONS, 2, 48, tokens), F32),
        pltpu.VMEM((16, tokens), F32),
        pltpu.VMEM((SIDE, 16, SIDE * TOK), F32),
        pltpu.VMEM((SIDE, 16, SIDE * TOK), F32),
        pltpu.VMEM((SIDE, EXPERTS, 256), F32),
        pltpu.VMEM((SIDE, EXPERTS, 256), F32),
        pltpu.VMEM((SIDE, EXPERTS, 128), F32),
        pltpu.VMEM((SIDE, EXPERTS, 128), F32),
        pltpu.VMEM((SIDE, SIDE, TOK, quarter), BF16),
        pltpu.VMEM((WINDOW * hidden_rows, 256), BF16),
        pltpu.VMEM((SIDE, 4, hidden_rows, tile), BF16),
        pltpu.VMEM((SIDE, 4, hidden_rows, tile), BF16),
        pltpu.VMEM((SIDE, SIDE, hidden_rows, tile), BF16),
        pltpu.VMEM((384, 384), BF16),
        pltpu.VMEM((256, 256), BF16),
        pltpu.VMEM((128, quarter), BF16),
        pltpu.VMEM((SIDE, SECTIONS, SIDE * CAP, quarter), BF16),
        pltpu.VMEM((SIDE, 2, SIDE * CAP // 2, quarter), BF16),
        pltpu.VMEM((2, SIDE, SECTIONS, SIDE * CAP, quarter), BF16),
        pltpu.VMEM((tile, half), F32),
        dma((3,)), dma((3,)),
        dma((7,)), dma((7,)),
        dma((4, 2)), dma((SIDE,)),
        dma((1,)), dma((SIDE,)),
        dma((7,)), dma((7,)),
        dma((SIDE,)), dma((SIDE,)),
        dma((7,)), dma((7,)),
        dma((7,)), dma((7,)),
        dma((1,)), dma((SIDE,)),
        dma((1,)), dma((SIDE, 2)),
        dma((1,)),
        dma((1,)), dma((SIDE,)),
        dma((1,)), dma((SIDE, 2)),
        dma((1,)), dma((SIDE,)),
    ]
    cotangent, down, router = pl.pallas_call(
        kernel,
        out_shape=(
            jax.ShapeDtypeStruct((tokens, half), BF16),
            jax.ShapeDtypeStruct((tile, half), BF16),
            jax.ShapeDtypeStruct((EXPERTS, 128), F32),
        ),
        in_specs=[vmem] * 7,
        out_specs=(vmem, vmem, vmem),
        scratch_shapes=scratch,
        compiler_params=pltpu.CompilerParams(
            collective_id=0, has_side_effects=True, vmem_limit_bytes=50 * 1024 * 1024
        ),
        cost_estimate=pl.CostEstimate(flops=8_000_000_000, bytes_accessed=8_000_000, transcendentals=0),
    )(
        top_cotangent,
        layer_inputs.reshape(tokens, half),
        router_weight[0].T,
        expert_ids.reshape(1, tokens * 2),
        expert_ids.reshape(tokens, 2).T.astype(F32),
        expert_outputs.reshape(tokens * 2, half),
        hidden.reshape(tokens * 2, half_ff),
    )
    return (
        cotangent.reshape(1, micro, tok, half),
        down.reshape(1, 1, 1, tile, half),
        router[:, :strip].T.reshape(1, 1, strip, EXPERTS),
    )


def solution(mesh):
    in_specs = (
        P(None, "ed", "tp"),
        P("section", None, "ed", "tp"),
        P("section", None, None),
        P("section", None, "ed", None),
        P("section", None, "ed", None, "tp"),
        P("section", None, "ed", None, "tp"),
    )
    out_specs = (
        P("section", None, "ed", "tp"),
        P("section", "tp", "ed", None, None),
        P("section", "tp", "ed", None),
    )
    return jax.shard_map(
        per_device, mesh=mesh, in_specs=in_specs, out_specs=out_specs, check_vma=False
    )
```

```python
import jax
import jax.numpy as jnp
from jax import lax
from jax.experimental import pallas as pl
from jax.experimental.pallas import tpu as pltpu
from jax.sharding import PartitionSpec as P

CAP = 12
MICRO = 4
TOK = 32
SIDE = 8
SECTIONS = 4
EXPERTS = 8
WINDOW = 4
HIGHEST = lax.Precision.HIGHEST
F32 = jnp.float32
BF16 = jnp.bfloat16
MESH = pl.DeviceIdType.MESH


def iota(shape, dim):
    return lax.broadcasted_iota(jnp.int32, shape, dim)


def divided(x, by):
    return ((x.astype(F32) + 0.5) * (1.0 / by)).astype(jnp.int32)


def contract(a, b, da, db, precision=None):
    return lax.dot_general(a, b, (((da,), (db,)), ((), ())), precision=precision, preferred_element_type=F32)


def split2(x):
    hi = x.astype(BF16)
    return hi, (x - hi.astype(F32)).astype(BF16)


def split3(x):
    hi = x.astype(BF16)
    rest = x - hi.astype(F32)
    mid = rest.astype(BF16)
    return hi, mid, (rest - mid.astype(F32)).astype(BF16)


def by_parts(x, rows, dims):
    parts = jnp.concatenate([p.astype(F32) for p in split3(x)], axis=0).astype(BF16)
    got = contract(parts, rows, 1, dims)
    n = x.shape[0]
    return got[:n] + got[n:2 * n] + got[2 * n:]


def earlier(segment_log2):
    r, c = iota((256, 256), 0), iota((256, 256), 1)
    same = jnp.right_shift(r, segment_log2) == jnp.right_shift(c, segment_log2)
    return jnp.where(same & (r < c), 1.0, 0.0).astype(BF16)


def kernel(
    top_ref, x_ref, w_ref, idr_ref, idt_ref, eo_ref, hid_ref,
    cot_ref, down_ref, router_ref,
    wb, pr, sm, szr, sg, ry, ryr, rz, rzr, topb, pick, hs, hy, hz, perm, seg, wq, xs, rel, sc, acc,
    w_s, w_r, p_s, p_r, tz_s, tz_r, ring_s, ring_r, sz_s, sz_r, sy_s, sy_r, ry_s, ry_r, rz_s, rz_r,
    hy_s, hy_r, hz_s, hz_r, hf_s, xx_s, xx_r, rr_s, rr_r, cc_s, cc_r,
):
    x = lax.axis_index("section")
    ed = lax.axis_index("ed")
    c = lax.axis_index("tp")
    y = ed // SIDE
    z = ed % SIDE
    half = top_ref.shape[2]
    quarter = half // 2
    own_half = z % 2
    own_expert = y // 2

    def at_x(k):
        return ((x + k) % SECTIONS, ed, c)

    def at_y(k):
        return (x, ((y + k) % SIDE) * SIDE + z, c)

    def at_z(k):
        return (x, y * SIDE + (z + k) % SIDE, c)

    partner = (x, ed, 1 - c)

    def off(i):
        return ((i + 1) // 2) * (1 - 2 * (i % 2))

    def source(i):
        return (y + SIDE + off(i)) % SIDE

    def copy(src, dst, send, recv, device):
        return pltpu.make_async_remote_copy(
            src_ref=src, dst_ref=dst, send_sem=send, recv_sem=recv, device_id=device, device_id_type=MESH
        )

    barrier = pltpu.get_barrier_semaphore()

    def greet(device):
        pl.semaphore_signal(barrier, inc=1, device_id=device, device_id_type=MESH)

    greet(partner)
    for k in range(1, SECTIONS):
        for cc in range(2):
            greet(((x + k) % SECTIONS, ed, cc))
    for k in range(1, SIDE):
        greet(at_y(k))
        for cc in range(2):
            greet((x, y * SIDE + (z + k) % SIDE, cc))

    ids_row = idr_ref[...]
    named = (jnp.broadcast_to(ids_row, (8, 256)) == iota((8, 256), 0)).astype(F32)
    rank = jnp.dot(named.astype(BF16), earlier(6), preferred_element_type=F32)
    r48 = iota((48, 256), 0)
    m48 = divided(r48, CAP)
    s48 = (r48 - CAP * m48).astype(F32)
    own_micro = m48 == jnp.right_shift(iota((48, 256), 1), 6)
    for e in range(WINDOW):
        hit = (
            (jnp.broadcast_to(named[e:e + 1], (48, 256)) > 0.5)
            & (jnp.broadcast_to(rank[e:e + 1], (48, 256)) == s48)
            & own_micro
        )
        pick[e * 48:(e + 1) * 48, :] = jnp.where(hit, 1.0, 0.0).astype(BF16)

    pl.semaphore_wait(barrier, 1 + 2 * (SECTIONS - 1) + 3 * (SIDE - 1))

    def w_copy(k):
        return copy(w_ref, wb.at[x], w_s.at[k - 1], w_r.at[k - 1], at_x(k))

    for k in range(1, SECTIONS):
        w_copy(k).start()
    wb[x] = w_ref[...]

    tilt = (z + c) % 2
    local = tilt == 0

    def tz_copy(r, cc):
        zd = (z + 2 * r + tilt) % SIDE
        return copy(
            top_ref.at[x, :, pl.ds(cc * quarter, quarter)], topb.at[y, z], tz_s.at[r, cc], tz_r.at[z],
            (x, y * SIDE + zd, cc),
        )

    for r in range(4):
        for cc in range(2):
            if r == 0:
                @pl.when(jnp.logical_not(local & (c == cc)))
                def _():
                    tz_copy(r, cc).start()
            else:
                tz_copy(r, cc).start()

    @pl.when(local)
    def _():
        topb[y, z] = top_ref[x, :, pl.ds(pl.multiple_of(c * quarter, 128), quarter)]

    def hidden_block(f, carry):
        cols = hid_ref[:, pl.ds(pl.multiple_of(f * 512, 512), 512)]
        got = jnp.dot(pick[...], cols, preferred_element_type=F32).astype(BF16)
        for e in range(WINDOW):
            hs[2 * e + f // 4, f % 4] = got[e * 48:(e + 1) * 48]
        return carry

    lax.fori_loop(0, 8, hidden_block, 0)

    def hy_copy(i):
        yd = (y + SIDE - off(i)) % SIDE
        return copy(hs.at[yd], hy.at[y], hy_s.at[0], hy_r.at[i], (x, yd * SIDE + z, c))

    def hy_start(i, carry):
        hy_copy(i).start()
        return carry

    def ring_copy(block, first, count, item, k):
        part = topb.at[block, pl.ds(first, count)]
        return copy(part, part, ring_s.at[0], ring_r.at[item], at_y(k))

    def tz_wait(zs, carry):
        @pl.when(jnp.logical_not(local & (zs == z)))
        def _():
            copy(topb.at[y, zs], topb.at[y, zs], tz_s.at[0, 0], tz_r.at[zs], partner).wait_recv()
        return carry

    lax.fori_loop(0, SIDE, tz_wait, 0)
    ring_copy(y, 0, SIDE, 1, 1).start()
    ring_copy(y, 0, SIDE, 2, SIDE - 1).start()
    lax.fori_loop(1, 3, hy_start, 0)
    hy[y] = hs[y]

    pair = z // 2
    parity = z % 2

    def hz_copy(i, d):
        ys = source(i)
        if d == 0:
            target, j = z + 1 - 2 * parity, 1
        elif d == 1:
            target, j = 2 * ((pair + 1) % 4), 0
        elif d == 2:
            target, j = 2 * ((pair + 2) % 4) + 1 - parity, 0
        else:
            target, j = 2 * ((pair + 3) % 4) + 1, 0
        return copy(
            hy.at[ys, (pair + d) % 4], hz.at[z, ys], hz_s.at[0], hz_r.at[i, j], (x, y * SIDE + target, c)
        )

    def send_hidden(i):
        ys = source(i)
        for d in (2, 1, 3, 0):
            hz_copy(i, d).start()
        hz[z, ys] = hy[ys, pair]

    near = 2 * ((pair + 3 + 2 * parity) % 4)
    far = 2 * ((pair + 2) % 4) + 1 - parity
    other = (x, y * SIDE + z + 1 - 2 * parity, c)

    def forward_hidden(i):
        ys = source(i)
        three = hz.at[pl.ds(0, 3), ys]
        copy(three, three, hz_s.at[0], hz_r.at[i, 0], partner).wait_recv()
        two, one = hz.at[pl.ds(near, 2), ys], hz.at[far, ys]
        copy(two, two, hf_s.at[0], hz_r.at[i, 1], other).start()
        copy(one, one, hf_s.at[0], hz_r.at[i, 1], other).start()

    def wait_hidden(i):
        four = hz.at[pl.ds(0, 4), source(i)]
        copy(four, four, hz_s.at[0], hz_r.at[i, 1], partner).wait_recv()

    send_hidden(0)

    core_cols = pl.ds(pl.multiple_of(c * half, 128), half)
    inputs = x_ref[...]
    top_tokens = top_ref[...].reshape(MICRO * TOK, half)
    outs = eo_ref[...]
    r128, c256 = iota((128, 256), 0), iota((128, 256), 1)
    pairs = jnp.where(c256 == 2 * r128, 1.0, jnp.where(c256 == 2 * r128 + 1, -1.0, 0.0))
    pr[x, c, 0:8] = by_parts(w_ref[:, core_cols], inputs, 1)
    products = contract(top_tokens, outs, 1, 1)
    dots = jnp.sum(products * jnp.abs(pairs), axis=0, keepdims=True)
    pr[x, c, 8:16] = contract(jnp.broadcast_to(dots, (8, 256)), pairs, 1, 1, HIGHEST)
    pr[x, c, 9:11] = idt_ref[...]

    def w_wait(k):
        copy(w_ref, wb.at[(x + SECTIONS - k) % SECTIONS], w_s.at[k - 1], w_r.at[k - 1], at_x(k)).wait_recv()

    for k in range(1, SECTIONS):
        w_wait(k)
    weights_half = wb[:, :, core_cols]
    crossed = by_parts(weights_half.reshape(SECTIONS * EXPERTS, half), outs, 1)
    pr[x, c, 16:48] = contract(crossed, pairs, 1, 1, HIGHEST)

    def p_copy(n):
        dx, dc = n // 2, n % 2
        return copy(pr.at[x, c], pr.at[x, c], p_s.at[n - 1], p_r.at[n - 1], ((x + dx) % SECTIONS, ed, (c + dc) % 2))

    for n in range(1, 2 * SECTIONS):
        p_copy(n).start()

    seg[...] = earlier(5)
    rp, cp = iota((384, 384), 0), iota((384, 384), 1)
    qp = divided(rp, CAP)
    perm[...] = jnp.where(
        cp == (qp & 7) * 48 + jnp.right_shift(qp, 3) * CAP + rp - CAP * qp, 1.0, 0.0
    ).astype(BF16)
    w_quarter = wb[:, :, pl.ds(pl.multiple_of(own_half * half + c * quarter, 128), quarter)]
    w_hi, w_mid = split2(w_quarter.reshape(SECTIONS * EXPERTS, quarter))
    wq[0:32] = w_hi
    wq[32:64] = w_hi
    wq[64:96] = w_mid
    wq[96:128] = jnp.zeros((32, quarter), BF16)
    ry[...] = jnp.zeros_like(ry)
    rz[...] = jnp.zeros_like(rz)

    for n in range(1, 2 * SECTIONS):
        dx, dc = n // 2, n % 2
        part = pr.at[(x + SECTIONS - dx) % SECTIONS, (c + dc) % 2]
        copy(part, part, p_s.at[n - 1], p_r.at[n - 1], partner).wait_recv()

    j8 = iota((8, 128), 0).astype(F32)
    firsts, grads, selects, dls = [], [None] * SECTIONS, [], [None] * SECTIONS
    for l in range(SECTIONS):
        logits = pr[l, 0, 0:8] + pr[l, 1, 0:8]
        id0, id1 = pr[l, 0, 9:10], pr[l, 0, 10:11]
        hot0 = jnp.where(jnp.broadcast_to(id0, (8, 128)) == j8, 1.0, 0.0)
        hot1 = jnp.where(jnp.broadcast_to(id1, (8, 128)) == j8, 1.0, 0.0)
        selects.append(hot0 - hot1)
        gap = jnp.sum(hot1 * logits, axis=0, keepdims=True) - jnp.sum(hot0 * logits, axis=0, keepdims=True)
        firsts.append(1.0 / (1.0 + jnp.exp(gap)))
        sm[4 + l:5 + l] = firsts[l]
        sm[8 + l:9 + l] = id0
        sm[12 + l:13 + l] = id1
    for l in range(SECTIONS - 1, -1, -1):
        total = pr[l, 0, 8:9] + pr[l, 1, 8:9]
        for a in range(l + 1, SECTIONS):
            cross = pr[l, 0, 16 + 8 * a:24 + 8 * a] + pr[l, 1, 16 + 8 * a:24 + 8 * a]
            total = total + grads[a] * jnp.sum(cross * selects[a], axis=0, keepdims=True)
        grads[l] = firsts[l] * (1.0 - firsts[l]) * total
        sm[l:l + 1] = grads[l]
        dls[l] = jnp.broadcast_to(grads[l], (8, 128)) * selects[l]

    to = iota((128, 256), 1) - z * TOK
    at = iota((128, 256), 0) - x * TOK
    put = jnp.where((to == at) & (to >= 0) & (to < TOK), 1.0, 0.0)
    szr[z] = jnp.dot(sm[...], put, precision=HIGHEST, preferred_element_type=F32)

    def sz_copy(k):
        return copy(szr.at[z], szr.at[z], sz_s.at[k - 1], sz_r.at[k - 1], at_z(k))

    for k in range(1, SIDE):
        sz_copy(k).start()

    def take_ring(i):
        part = topb.at[source(i)]
        copy(part, part, ring_s.at[0], ring_r.at[i], partner).wait_recv()

        @pl.when(i < 5)
        def _():
            ring_copy(source(i), 0, SIDE, i + 2, 1 + (1 - i % 2) * (SIDE - 2)).start()

        @pl.when(i == 5)
        def _():
            ring_copy(source(i), 0, 4, SIDE - 1, 1).start()

        @pl.when(i == 6)
        def _():
            ring_copy(source(i), 4, 4, SIDE - 1, SIDE - 1).start()

        @pl.when(i < SIDE - 2)
        def _():
            hy_copy(i + 2).start()

    own_dl = jnp.zeros((8, 128), F32)
    for l in range(SECTIONS):
        own_dl = jnp.where(x == l, dls[l], own_dl)
    router_part = by_parts(own_dl, inputs, 0)
    strip = half // SIDE
    for k in range(SIDE):
        ry[k, :, 0:strip] = router_part[:, k * strip:(k + 1) * strip]

    def ry_copy(k):
        yd = (y + k) % SIDE
        return copy(ry.at[yd], ryr.at[y], ry_s.at[k - 1], ry_r.at[k - 1], at_y(k))

    for k in range(1, SIDE):
        ry_copy(k).start()
    ryr[y] = ry[y]

    def first_rings(i, carry):
        take_ring(i)
        return carry

    lax.fori_loop(1, 3, first_rings, 0)

    for k in range(1, SIDE):
        part = szr.at[(z + SIDE - k) % SIDE]
        copy(part, part, sz_s.at[k - 1], sz_r.at[k - 1], partner).wait_recv()
    total = szr[0]
    for k in range(1, SIDE):
        total = total + szr[k]
    sg[y] = total

    def sy_copy(i):
        return copy(sg.at[y], sg.at[y], sy_s.at[i], sy_r.at[i], at_y(SIDE - off(i)))

    for i in range(1, SIDE):
        sy_copy(i).start()

    def rz_copy(k):
        zd = (z + k) % SIDE
        return copy(rz.at[zd], rzr.at[z], rz_s.at[k - 1], rz_r.at[k - 1], at_z(k))

    def router_second():
        for k in range(1, SIDE):
            part = ryr.at[(y + SIDE - k) % SIDE]
            copy(part, part, ry_s.at[k - 1], ry_r.at[k - 1], partner).wait_recv()
        total = ryr[0]
        for k in range(1, SIDE):
            total = total + ryr[k]
        piece = strip // SIDE
        for k in range(SIDE):
            rz[k, :, 0:piece] = total[:, k * piece:(k + 1) * piece]
        for k in range(1, SIDE):
            rz_copy(k).start()
        rzr[z] = rz[z]

    def cotangents():
        cotangent = top_tokens
        for l in range(SECTIONS - 1, -1, -1):
            d_hi, d_mid, _ = split3(dls[l])
            w_hi, w_mid, _ = split3(wb[l, :, core_cols])
            left = jnp.concatenate([d.astype(F32) for d in (d_hi, d_mid, d_hi)], axis=0).astype(BF16)
            right = jnp.concatenate([w.astype(F32) for w in (w_hi, w_hi, w_mid)], axis=0).astype(BF16)
            step = contract(left, right, 0, 0)
            cotangent = jnp.where(l >= x, (cotangent.astype(F32) + step).astype(BF16), cotangent)
        cot_ref[...] = cotangent

    def take_hidden(i):
        copy(hs.at[0], hy.at[source(i)], hy_s.at[0], hy_r.at[i], partner).wait_recv()
        send_hidden(i)

    def x_copy(i, n):
        ys = source(i)
        if n < 2:
            k = 1 + 2 * n
            return copy(
                xs.at[i, (x + k) % SECTIONS], sc.at[c, ys, x], xx_s.at[0], xx_r.at[i], at_x(k)
            )
        n -= 2
        return copy(
            xs.at[i, (x + 2) % SECTIONS, pl.ds(48 * n, 48)], rel.at[i, n], xx_s.at[0], rr_r.at[i, n],
            at_x(1 + 2 * n),
        )

    def relay_copy(i, n):
        k = 1 + 2 * n
        return copy(
            rel.at[i, n], sc.at[c, source(i), (x + SECTIONS - k) % SECTIONS, pl.ds(48 * n, 48)],
            rr_s.at[0], xx_r.at[i], at_x(k),
        )

    def relay(i):
        for n in range(2):
            copy(rel.at[i, n], rel.at[i, n], rr_s.at[0], rr_r.at[i, n], partner).wait_recv()
            relay_copy(i, n).start()

    def core_copy(i):
        part = sc.at[c, source(i)]
        return copy(part, part, cc_s.at[0], cc_r.at[i], partner)

    r96 = iota((96, 256), 0)
    z96 = divided(r96, CAP)
    s96 = (r96 - CAP * z96).astype(F32)
    own_block = z96 == jnp.right_shift(iota((96, 256), 1), 5)
    mine = own_expert.astype(F32)

    def select(i):
        ys = source(i)
        small = sg[ys]
        grad, first, id0, id1 = small[0:4], small[4:8], small[8:12], small[12:16]
        is0, is1 = id0 == mine, id1 == mine
        named = jnp.where(is0 | is1, 1.0, 0.0)
        gate = jnp.where(is0, first, 1.0 - first)
        rank = jnp.dot(
            jnp.concatenate([named, named], axis=0).astype(BF16), seg[...], preferred_element_type=F32
        )
        dl = []
        jt = iota((8, 256), 0).astype(F32)
        for l in range(SECTIONS):
            sel = jnp.where(jnp.broadcast_to(id0[l:l + 1], (8, 256)) == jt, 1.0, 0.0)
            sel = sel - jnp.where(jnp.broadcast_to(id1[l:l + 1], (8, 256)) == jt, 1.0, 0.0)
            dl.append(jnp.broadcast_to(grad[l:l + 1], (8, 256)) * sel)
        d_hi, d_mid = split2(jnp.concatenate(dl, axis=0))
        side = jnp.concatenate([d_hi, d_mid, d_hi, jnp.zeros_like(d_hi)], axis=0)
        tops = topb[ys].reshape(SIDE * TOK, quarter)
        places, gates = [], []
        for l in range(SECTIONS):
            hit = (
                (jnp.broadcast_to(named[l:l + 1], (96, 256)) > 0.5)
                & (jnp.broadcast_to(rank[l:l + 1], (96, 256)) == s96)
                & own_block
            )
            gates.append(jnp.sum(
                jnp.where(hit, jnp.broadcast_to(gate[l:l + 1], (96, 256)), 0.0), axis=1, keepdims=True
            ))
            places.append(jnp.where(hit, 1.0, 0.0).astype(BF16))
        place = jnp.concatenate(places, axis=0)
        lefts = contract(place, side, 1, 1)
        above = jnp.right_shift(iota((96, 128), 1) & 31, 3)
        left = jnp.concatenate(
            [jnp.where(above > l, lefts[96 * l:96 * (l + 1)], 0.0).astype(BF16) for l in range(SECTIONS)], axis=0
        )
        rows = jnp.dot(place, tops, preferred_element_type=F32)
        rows = rows + jnp.dot(left, wq[...], preferred_element_type=F32)
        for l in range(SECTIONS):
            xs[i, l] = (gates[l] * rows[96 * l:96 * (l + 1)]).astype(BF16)
        for n in (2, 3, 0, 1):
            x_copy(i, n).start()
        sc[c, ys, x] = xs[i, x]

    def to_partner(i):
        three = sc.at[c, source(i), pl.ds(0, 3)]
        copy(three, three, xx_s.at[0], xx_r.at[i], partner).wait_recv()
        core_copy(i).start()

    def accumulate(i):
        ys = source(i)
        wait_hidden(i)
        part = sc.at[1 - c, ys]
        copy(part, part, cc_s.at[0], cc_r.at[i], partner).wait_recv()
        rows = jnp.dot(perm[...], hz[:, ys].reshape(384, 512), preferred_element_type=F32).astype(BF16)
        for q in range(2):
            cols = slice(q * quarter, (q + 1) * quarter)
            acc[:, cols] += contract(rows, sc[q, ys].reshape(384, quarter), 0, 0)

    acc[...] = jnp.zeros_like(acc)

    def small_wait(i):
        copy(sg.at[source(i)], sg.at[source(i)], sy_s.at[i], sy_r.at[i], partner).wait_recv()

    def body(i, carry):
        @pl.when(i < 3)
        def _():
            forward_hidden(i)

        @pl.when((i >= 4) & (i < SIDE + 1))
        def _():
            forward_hidden(i - 1)

        @pl.when((i >= 3) & (i < SIDE) & (i % 2 == 1))
        def _():
            take_ring(i)

        @pl.when((i >= 3) & (i < SIDE - 1) & (i % 2 == 1))
        def _():
            take_ring(i + 1)

        @pl.when((i >= 1) & (i < SIDE))
        def _():
            small_wait(i)

        @pl.when(i < SIDE)
        def _():
            select(i)

        @pl.when(i < 2)
        def _():
            take_hidden(i + 1)

        @pl.when((i >= 3) & (i < SIDE))
        def _():
            take_hidden(i)

        @pl.when((i >= 1) & (i < SIDE + 1))
        def _():
            relay(i - 1)

        @pl.when((i >= 2) & (i < SIDE + 2))
        def _():
            to_partner(i - 2)

        @pl.when(i == 2)
        def _():
            router_second()

        @pl.when(i == 1)
        def _():
            cotangents()

        @pl.when(i >= 3)
        def _():
            accumulate(i - 3)

        return carry

    lax.fori_loop(0, SIDE + 3, body, 0)
    down_ref[...] = acc[...].astype(BF16)
    for k in range(1, SIDE):
        part = rzr.at[(z + SIDE - k) % SIDE]
        copy(part, part, rz_s.at[k - 1], rz_r.at[k - 1], partner).wait_recv()
    total = rzr[0]
    for k in range(1, SIDE):
        total = total + rzr[k]
    router_ref[...] = total

    for k in range(1, SECTIONS):
        w_copy(k).wait_send()
    for n in range(1, 2 * SECTIONS):
        p_copy(n).wait_send()
    for r in range(4):
        for cc in range(2):
            if r == 0:
                @pl.when(jnp.logical_not(local & (c == cc)))
                def _():
                    tz_copy(r, cc).wait_send()
            else:
                tz_copy(r, cc).wait_send()
    for k in range(1, SIDE):
        sz_copy(k).wait_send()
        sy_copy(k).wait_send()
        ry_copy(k).wait_send()
        rz_copy(k).wait_send()


    def drained(ref, sem):
        copy(ref, ref, sem.at[0], cc_r.at[0], partner).wait_send()

    drained(topb.at[pl.ds(0, SIDE - 1)], ring_s)
    drained(hy.at[pl.ds(0, SIDE - 1)], hy_s)
    drained(hy, hz_s)
    drained(hy.at[:, pl.ds(0, 3)], hf_s)
    drained(xs.at[:, pl.ds(0, 3)], xx_s)
    drained(rel, rr_s)
    drained(xs, cc_s)


def per_device(top_cotangent, layer_inputs, router_weight, expert_ids, expert_outputs, hidden):
    micro, tok, half = top_cotangent.shape
    tokens = micro * tok
    half_ff = hidden.shape[4]
    width = router_weight.shape[1]
    quarter = half // 2
    tile = half_ff // SIDE
    strip = half // SIDE // SIDE
    vmem = pl.BlockSpec(memory_space=pltpu.VMEM)
    dma = pltpu.SemaphoreType.DMA
    hidden_rows = MICRO * CAP
    scratch = [
        pltpu.VMEM((SECTIONS, EXPERTS, width), F32),
        pltpu.VMEM((SECTIONS, 2, 48, tokens), F32),
        pltpu.VMEM((16, tokens), F32),
        pltpu.VMEM((SIDE, 16, SIDE * TOK), F32),
        pltpu.VMEM((SIDE, 16, SIDE * TOK), F32),
        pltpu.VMEM((SIDE, EXPERTS, 256), F32),
        pltpu.VMEM((SIDE, EXPERTS, 256), F32),
        pltpu.VMEM((SIDE, EXPERTS, 128), F32),
        pltpu.VMEM((SIDE, EXPERTS, 128), F32),
        pltpu.VMEM((SIDE, SIDE, TOK, quarter), BF16),
        pltpu.VMEM((WINDOW * hidden_rows, 256), BF16),
        pltpu.VMEM((SIDE, 4, hidden_rows, tile), BF16),
        pltpu.VMEM((SIDE, 4, hidden_rows, tile), BF16),
        pltpu.VMEM((SIDE, SIDE, hidden_rows, tile), BF16),
        pltpu.VMEM((384, 384), BF16),
        pltpu.VMEM((256, 256), BF16),
        pltpu.VMEM((128, quarter), BF16),
        pltpu.VMEM((SIDE, SECTIONS, SIDE * CAP, quarter), BF16),
        pltpu.VMEM((SIDE, 2, SIDE * CAP // 2, quarter), BF16),
        pltpu.VMEM((2, SIDE, SECTIONS, SIDE * CAP, quarter), BF16),
        pltpu.VMEM((tile, half), F32),
        dma((3,)), dma((3,)),
        dma((7,)), dma((7,)),
        dma((4, 2)), dma((SIDE,)),
        dma((1,)), dma((SIDE,)),
        dma((7,)), dma((7,)),
        dma((SIDE,)), dma((SIDE,)),
        dma((7,)), dma((7,)),
        dma((7,)), dma((7,)),
        dma((1,)), dma((SIDE,)),
        dma((1,)), dma((SIDE, 2)),
        dma((1,)),
        dma((1,)), dma((SIDE,)),
        dma((1,)), dma((SIDE, 2)),
        dma((1,)), dma((SIDE,)),
    ]
    cotangent, down, router = pl.pallas_call(
        kernel,
        out_shape=(
            jax.ShapeDtypeStruct((tokens, half), BF16),
            jax.ShapeDtypeStruct((tile, half), BF16),
            jax.ShapeDtypeStruct((EXPERTS, 128), F32),
        ),
        in_specs=[vmem] * 7,
        out_specs=(vmem, vmem, vmem),
        scratch_shapes=scratch,
        compiler_params=pltpu.CompilerParams(
            collective_id=0, has_side_effects=True, vmem_limit_bytes=50 * 1024 * 1024
        ),
        cost_estimate=pl.CostEstimate(flops=8_000_000_000, bytes_accessed=8_000_000, transcendentals=0),
    )(
        top_cotangent,
        layer_inputs.reshape(tokens, half),
        router_weight[0].T,
        expert_ids.reshape(1, tokens * 2),
        expert_ids.reshape(tokens, 2).T.astype(F32),
        expert_outputs.reshape(tokens * 2, half),
        hidden.reshape(tokens * 2, half_ff),
    )
    return (
        cotangent.reshape(1, micro, tok, half),
        down.reshape(1, 1, 1, tile, half),
        router[:, :strip].T.reshape(1, 1, strip, EXPERTS),
    )


def solution(mesh):
    in_specs = (
        P(None, "ed", "tp"),
        P("section", None, "ed", "tp"),
        P("section", None, None),
        P("section", None, "ed", None),
        P("section", None, "ed", None, "tp"),
        P("section", None, "ed", None, "tp"),
    )
    out_specs = (
        P("section", None, "ed", "tp"),
        P("section", "tp", "ed", None, None),
        P("section", "tp", "ed", None),
    )
    return jax.shard_map(
        per_device, mesh=mesh, in_specs=in_specs, out_specs=out_specs, check_vma=False
    )
```

```python
import jax
import jax.numpy as jnp
from jax import lax
from jax.experimental import pallas as pl
from jax.experimental.pallas import tpu as pltpu
from jax.sharding import PartitionSpec as P

CAP = 12
MICRO = 4
TOK = 32
SIDE = 8
SECTIONS = 4
EXPERTS = 8
WINDOW = 4
HIGHEST = lax.Precision.HIGHEST
F32 = jnp.float32
BF16 = jnp.bfloat16
MESH = pl.DeviceIdType.MESH


def iota(shape, dim):
    return lax.broadcasted_iota(jnp.int32, shape, dim)


def divided(x, by):
    return ((x.astype(F32) + 0.5) * (1.0 / by)).astype(jnp.int32)


def contract(a, b, da, db, precision=None):
    return lax.dot_general(a, b, (((da,), (db,)), ((), ())), precision=precision, preferred_element_type=F32)


def split2(x):
    hi = x.astype(BF16)
    return hi, (x - hi.astype(F32)).astype(BF16)


def split3(x):
    hi = x.astype(BF16)
    rest = x - hi.astype(F32)
    mid = rest.astype(BF16)
    return hi, mid, (rest - mid.astype(F32)).astype(BF16)


def by_parts(x, rows, dims):
    parts = jnp.concatenate([p.astype(F32) for p in split3(x)], axis=0).astype(BF16)
    got = contract(parts, rows, 1, dims)
    n = x.shape[0]
    return got[:n] + got[n:2 * n] + got[2 * n:]


def earlier(segment_log2):
    r, c = iota((256, 256), 0), iota((256, 256), 1)
    same = jnp.right_shift(r, segment_log2) == jnp.right_shift(c, segment_log2)
    return jnp.where(same & (r < c), 1.0, 0.0).astype(BF16)


def kernel(
    top_ref, x_ref, w_ref, ids_ref, eo_ref, hid_ref,
    cot_ref, down_ref, router_ref,
    wb, pr, sm, szr, sg, ry, ryr, rz, rzr, topb, pick, hs, hy, hz, perm, seg, wq, xs, rel, sc, acc, hv, hv_sem,
    w_s, w_r, p_s, p_r, tz_s, tz_r, ring_s, ring_r, sz_s, sz_r, sy_s, sy_r, ry_s, ry_r, rz_s, rz_r,
    hy_s, hy_r, hz_s, hz_r, hf_s, xx_s, xx_r, rr_s, rr_r, cc_s, cc_r,
):
    x = lax.axis_index("section")
    ed = lax.axis_index("ed")
    c = lax.axis_index("tp")
    y = ed // SIDE
    z = ed % SIDE
    half = top_ref.shape[2]
    quarter = half // 2
    own_half = z % 2
    own_expert = y // 2

    def at_x(k):
        return ((x + k) % SECTIONS, ed, c)

    def at_y(k):
        return (x, ((y + k) % SIDE) * SIDE + z, c)

    def at_z(k):
        return (x, y * SIDE + (z + k) % SIDE, c)

    partner = (x, ed, 1 - c)

    def off(i):
        return ((i + 1) // 2) * (1 - 2 * (i % 2))

    def source(i):
        return (y + SIDE + off(i)) % SIDE

    def copy(src, dst, send, recv, device):
        return pltpu.make_async_remote_copy(
            src_ref=src, dst_ref=dst, send_sem=send, recv_sem=recv, device_id=device, device_id_type=MESH
        )

    barrier = pltpu.get_barrier_semaphore()

    def greet(device):
        pl.semaphore_signal(barrier, inc=1, device_id=device, device_id_type=MESH)

    greet(partner)
    for k in range(1, SECTIONS):
        for cc in range(2):
            greet(((x + k) % SECTIONS, ed, cc))
    for k in range(1, SIDE):
        greet(at_y(k))
        for cc in range(2):
            greet((x, y * SIDE + (z + k) % SIDE, cc))

    load = pltpu.make_async_copy(hid_ref, hv, hv_sem.at[0])
    load.start()

    ids = ids_ref[...].astype(F32).astype(BF16)
    route = iota((8, 256), 1)
    spread = (jnp.right_shift(iota((TOK, 256), 1), 1) & (TOK - 1)) == iota((TOK, 256), 0)
    wide = jnp.dot(ids, jnp.where(spread, 1.0, 0.0).astype(BF16), preferred_element_type=F32)
    own_row = iota((8, 256), 0) == 2 * jnp.right_shift(route, 6) + (route & 1)
    ids_row = jnp.sum(jnp.where(own_row, wide, 0.0), axis=0, keepdims=True)
    spread = (iota((TOK, 128), 1) & (TOK - 1)) == iota((TOK, 128), 0)
    wide = jnp.dot(ids, jnp.where(spread, 1.0, 0.0).astype(BF16), preferred_element_type=F32)
    first_row = iota((8, 128), 0) - 2 * jnp.right_shift(iota((8, 128), 1), 5)
    ids_first = jnp.sum(jnp.where(first_row == 0, wide, 0.0), axis=0, keepdims=True)
    ids_second = jnp.sum(jnp.where(first_row == 1, wide, 0.0), axis=0, keepdims=True)
    named = (jnp.broadcast_to(ids_row, (8, 256)) == iota((8, 256), 0).astype(F32)).astype(F32)
    rank = jnp.dot(named.astype(BF16), earlier(6), preferred_element_type=F32)
    r48 = iota((48, 256), 0)
    m48 = divided(r48, CAP)
    s48 = (r48 - CAP * m48).astype(F32)
    own_micro = m48 == jnp.right_shift(iota((48, 256), 1), 6)
    for e in range(WINDOW):
        hit = (
            (jnp.broadcast_to(named[e:e + 1], (48, 256)) > 0.5)
            & (jnp.broadcast_to(rank[e:e + 1], (48, 256)) == s48)
            & own_micro
        )
        pick[e * 48:(e + 1) * 48, :] = jnp.where(hit, 1.0, 0.0).astype(BF16)

    pl.semaphore_wait(barrier, 1 + 2 * (SECTIONS - 1) + 3 * (SIDE - 1))

    def w_copy(k):
        return copy(w_ref, wb.at[x], w_s.at[k - 1], w_r.at[k - 1], at_x(k))

    for k in range(1, SECTIONS):
        w_copy(k).start()
    wb[x] = w_ref[...]

    tilt = (z + c) % 2
    local = tilt == 0

    def tz_copy(r, cc):
        zd = (z + 2 * r + tilt) % SIDE
        return copy(
            top_ref.at[x, :, pl.ds(cc * quarter, quarter)], topb.at[y, z], tz_s.at[r, cc], tz_r.at[z],
            (x, y * SIDE + zd, cc),
        )

    for r in range(4):
        for cc in range(2):
            if r == 0:
                @pl.when(jnp.logical_not(local & (c == cc)))
                def _():
                    tz_copy(r, cc).start()
            else:
                tz_copy(r, cc).start()

    @pl.when(local)
    def _():
        topb[y, z] = top_ref[x, :, pl.ds(pl.multiple_of(c * quarter, 128), quarter)]

    def hidden_block(f, carry):
        cols = hv[:, :, pl.ds(pl.multiple_of(f * 512, 512), 512)].reshape(256, 512)
        got = jnp.dot(pick[...], cols, preferred_element_type=F32).astype(BF16)
        for e in range(WINDOW):
            hs[2 * e + f // 4, f % 4] = got[e * 48:(e + 1) * 48]
        return carry

    load.wait()
    lax.fori_loop(0, 8, hidden_block, 0)

    def hy_copy(i):
        yd = (y + SIDE - off(i)) % SIDE
        return copy(hs.at[yd], hy.at[y], hy_s.at[0], hy_r.at[i], (x, yd * SIDE + z, c))

    def hy_start(i, carry):
        hy_copy(i).start()
        return carry

    def ring_copy(block, first, count, item, k):
        part = topb.at[block, pl.ds(first, count)]
        return copy(part, part, ring_s.at[0], ring_r.at[item], at_y(k))

    def tz_wait(zs, carry):
        @pl.when(jnp.logical_not(local & (zs == z)))
        def _():
            copy(topb.at[y, zs], topb.at[y, zs], tz_s.at[0, 0], tz_r.at[zs], partner).wait_recv()
        return carry

    lax.fori_loop(0, SIDE, tz_wait, 0)
    ring_copy(y, 0, SIDE, 1, 1).start()
    ring_copy(y, 0, SIDE, 2, SIDE - 1).start()
    lax.fori_loop(1, 5, hy_start, 0)
    hy[y] = hs[y]

    pair = z // 2
    parity = z % 2

    def hz_copy(i, d):
        ys = source(i)
        if d == 0:
            target, j = z + 1 - 2 * parity, 1
        elif d == 1:
            target, j = 2 * ((pair + 1) % 4), 0
        elif d == 2:
            target, j = 2 * ((pair + 2) % 4) + 1 - parity, 0
        else:
            target, j = 2 * ((pair + 3) % 4) + 1, 0
        return copy(
            hy.at[ys, (pair + d) % 4], hz.at[z, ys], hz_s.at[0], hz_r.at[i, j], (x, y * SIDE + target, c)
        )

    def send_hidden(i):
        ys = source(i)
        for d in (2, 1, 3, 0):
            hz_copy(i, d).start()
        hz[z, ys] = hy[ys, pair]

    near = 2 * ((pair + 3 + 2 * parity) % 4)
    far = 2 * ((pair + 2) % 4) + 1 - parity
    other = (x, y * SIDE + z + 1 - 2 * parity, c)

    def forward_hidden(i):
        ys = source(i)
        three = hz.at[pl.ds(0, 3), ys]
        copy(three, three, hz_s.at[0], hz_r.at[i, 0], partner).wait_recv()
        two, one = hz.at[pl.ds(near, 2), ys], hz.at[far, ys]
        copy(two, two, hf_s.at[0], hz_r.at[i, 1], other).start()
        copy(one, one, hf_s.at[0], hz_r.at[i, 1], other).start()

    def wait_hidden(i):
        four = hz.at[pl.ds(0, 4), source(i)]
        copy(four, four, hz_s.at[0], hz_r.at[i, 1], partner).wait_recv()

    send_hidden(0)

    core_cols = pl.ds(pl.multiple_of(c * half, 128), half)
    inputs = x_ref[...]
    top_tokens = top_ref[...].reshape(MICRO * TOK, half)
    outs = eo_ref[...].reshape(256, half)
    r128, c256 = iota((128, 256), 0), iota((128, 256), 1)
    pairs = jnp.where(c256 == 2 * r128, 1.0, jnp.where(c256 == 2 * r128 + 1, -1.0, 0.0))
    pr[x, c, 0:8] = by_parts(w_ref[:, core_cols], inputs, 1)
    products = contract(top_tokens, outs, 1, 1)
    dots = jnp.sum(products * jnp.abs(pairs), axis=0, keepdims=True)
    dots = contract(jnp.broadcast_to(dots, (8, 256)), pairs, 1, 1, HIGHEST)
    lines = iota((8, 128), 0)
    pr[x, c, 8:16] = jnp.where(lines == 1, ids_first, jnp.where(lines == 2, ids_second, dots))

    def w_wait(k):
        copy(w_ref, wb.at[(x + SECTIONS - k) % SECTIONS], w_s.at[k - 1], w_r.at[k - 1], at_x(k)).wait_recv()

    for k in range(1, SECTIONS):
        w_wait(k)
    weights_half = wb[:, :, core_cols]
    crossed = by_parts(weights_half.reshape(SECTIONS * EXPERTS, half), outs, 1)
    pr[x, c, 16:48] = contract(crossed, pairs, 1, 1, HIGHEST)

    def p_copy(n):
        dx, dc = n // 2, n % 2
        return copy(pr.at[x, c], pr.at[x, c], p_s.at[n - 1], p_r.at[n - 1], ((x + dx) % SECTIONS, ed, (c + dc) % 2))

    for n in range(1, 2 * SECTIONS):
        p_copy(n).start()

    seg[...] = earlier(5)
    rp, cp = iota((384, 384), 0), iota((384, 384), 1)
    qp = divided(rp, CAP)
    perm[...] = jnp.where(
        cp == (qp & 7) * 48 + jnp.right_shift(qp, 3) * CAP + rp - CAP * qp, 1.0, 0.0
    ).astype(BF16)
    w_quarter = wb[:, :, pl.ds(pl.multiple_of(own_half * half + c * quarter, 128), quarter)]
    w_hi, w_mid = split2(w_quarter.reshape(SECTIONS * EXPERTS, quarter))
    wq[0:32] = w_hi
    wq[32:64] = w_hi
    wq[64:96] = w_mid
    wq[96:128] = jnp.zeros((32, quarter), BF16)
    ry[...] = jnp.zeros_like(ry)
    rz[...] = jnp.zeros_like(rz)

    for n in range(1, 2 * SECTIONS):
        dx, dc = n // 2, n % 2
        part = pr.at[(x + SECTIONS - dx) % SECTIONS, (c + dc) % 2]
        copy(part, part, p_s.at[n - 1], p_r.at[n - 1], partner).wait_recv()

    j8 = iota((8, 128), 0).astype(F32)
    firsts, grads, selects, dls = [], [None] * SECTIONS, [], [None] * SECTIONS
    for l in range(SECTIONS):
        logits = pr[l, 0, 0:8] + pr[l, 1, 0:8]
        id0, id1 = pr[l, 0, 9:10], pr[l, 0, 10:11]
        hot0 = jnp.where(jnp.broadcast_to(id0, (8, 128)) == j8, 1.0, 0.0)
        hot1 = jnp.where(jnp.broadcast_to(id1, (8, 128)) == j8, 1.0, 0.0)
        selects.append(hot0 - hot1)
        gap = jnp.sum(hot1 * logits, axis=0, keepdims=True) - jnp.sum(hot0 * logits, axis=0, keepdims=True)
        firsts.append(1.0 / (1.0 + jnp.exp(gap)))
        sm[4 + l:5 + l] = firsts[l]
        sm[8 + l:9 + l] = id0
        sm[12 + l:13 + l] = id1
    for l in range(SECTIONS - 1, -1, -1):
        total = pr[l, 0, 8:9] + pr[l, 1, 8:9]
        for a in range(l + 1, SECTIONS):
            cross = pr[l, 0, 16 + 8 * a:24 + 8 * a] + pr[l, 1, 16 + 8 * a:24 + 8 * a]
            total = total + grads[a] * jnp.sum(cross * selects[a], axis=0, keepdims=True)
        grads[l] = firsts[l] * (1.0 - firsts[l]) * total
        sm[l:l + 1] = grads[l]
        dls[l] = jnp.broadcast_to(grads[l], (8, 128)) * selects[l]

    to = iota((128, 256), 1) - z * TOK
    at = iota((128, 256), 0) - x * TOK
    put = jnp.where((to == at) & (to >= 0) & (to < TOK), 1.0, 0.0)
    szr[z] = jnp.dot(sm[...], put, precision=HIGHEST, preferred_element_type=F32)

    def sz_copy(k):
        return copy(szr.at[z], szr.at[z], sz_s.at[k - 1], sz_r.at[k - 1], at_z(k))

    for k in range(1, SIDE):
        sz_copy(k).start()

    def take_ring(i):
        part = topb.at[source(i)]
        copy(part, part, ring_s.at[0], ring_r.at[i], partner).wait_recv()

        @pl.when(i < 5)
        def _():
            ring_copy(source(i), 0, SIDE, i + 2, 1 + (1 - i % 2) * (SIDE - 2)).start()

        @pl.when(i == 5)
        def _():
            ring_copy(source(i), 0, 4, SIDE - 1, 1).start()

        @pl.when(i == 6)
        def _():
            ring_copy(source(i), 4, 4, SIDE - 1, SIDE - 1).start()

        @pl.when(i < 4)
        def _():
            hy_copy(i + 4).start()

    own_dl = jnp.zeros((8, 128), F32)
    for l in range(SECTIONS):
        own_dl = jnp.where(x == l, dls[l], own_dl)
    router_part = by_parts(own_dl, inputs, 0)
    strip = half // SIDE
    for k in range(SIDE):
        ry[k, :, 0:strip] = router_part[:, k * strip:(k + 1) * strip]

    def ry_copy(k):
        yd = (y + k) % SIDE
        return copy(ry.at[yd], ryr.at[y], ry_s.at[k - 1], ry_r.at[k - 1], at_y(k))

    for k in range(1, SIDE):
        ry_copy(k).start()
    ryr[y] = ry[y]


    for k in range(1, SIDE):
        part = szr.at[(z + SIDE - k) % SIDE]
        copy(part, part, sz_s.at[k - 1], sz_r.at[k - 1], partner).wait_recv()
    total = szr[0]
    for k in range(1, SIDE):
        total = total + szr[k]
    sg[y] = total

    def sy_copy(i):
        return copy(sg.at[y], sg.at[y], sy_s.at[i], sy_r.at[i], at_y(SIDE - off(i)))

    for i in range(1, SIDE):
        sy_copy(i).start()

    def first_rings(i, carry):
        take_ring(i)
        return carry

    lax.fori_loop(1, 3, first_rings, 0)

    def rz_copy(k):
        zd = (z + k) % SIDE
        return copy(rz.at[zd], rzr.at[z], rz_s.at[k - 1], rz_r.at[k - 1], at_z(k))

    def router_second():
        for k in range(1, SIDE):
            part = ryr.at[(y + SIDE - k) % SIDE]
            copy(part, part, ry_s.at[k - 1], ry_r.at[k - 1], partner).wait_recv()
        total = ryr[0]
        for k in range(1, SIDE):
            total = total + ryr[k]
        piece = strip // SIDE
        for k in range(SIDE):
            rz[k, :, 0:piece] = total[:, k * piece:(k + 1) * piece]
        for k in range(1, SIDE):
            rz_copy(k).start()
        rzr[z] = rz[z]

    def cotangents():
        cotangent = top_tokens
        for l in range(SECTIONS - 1, -1, -1):
            d_hi, d_mid, _ = split3(dls[l])
            w_hi, w_mid, _ = split3(wb[l, :, core_cols])
            left = jnp.concatenate([d.astype(F32) for d in (d_hi, d_mid, d_hi)], axis=0).astype(BF16)
            right = jnp.concatenate([w.astype(F32) for w in (w_hi, w_hi, w_mid)], axis=0).astype(BF16)
            step = contract(left, right, 0, 0)
            cotangent = jnp.where(l >= x, (cotangent.astype(F32) + step).astype(BF16), cotangent)
        cot_ref[...] = cotangent

    def take_hidden(i):
        copy(hs.at[0], hy.at[source(i)], hy_s.at[0], hy_r.at[i], partner).wait_recv()
        send_hidden(i)

    def x_copy(i, n):
        ys = source(i)
        if n < 2:
            k = 1 + 2 * n
            return copy(
                xs.at[i, (x + k) % SECTIONS], sc.at[c, ys, x], xx_s.at[0], xx_r.at[i], at_x(k)
            )
        n -= 2
        return copy(
            xs.at[i, (x + 2) % SECTIONS, pl.ds(48 * n, 48)], rel.at[i, n], xx_s.at[0], rr_r.at[i, n],
            at_x(1 + 2 * n),
        )

    def relay_copy(i, n):
        k = 1 + 2 * n
        return copy(
            rel.at[i, n], sc.at[c, source(i), (x + SECTIONS - k) % SECTIONS, pl.ds(48 * n, 48)],
            rr_s.at[0], xx_r.at[i], at_x(k),
        )

    def relay(i):
        for n in range(2):
            copy(rel.at[i, n], rel.at[i, n], rr_s.at[0], rr_r.at[i, n], partner).wait_recv()
            relay_copy(i, n).start()

    def core_copy(i):
        part = sc.at[c, source(i)]
        return copy(part, part, cc_s.at[0], cc_r.at[i], partner)

    r96 = iota((96, 256), 0)
    z96 = divided(r96, CAP)
    s96 = (r96 - CAP * z96).astype(F32)
    own_block = z96 == jnp.right_shift(iota((96, 256), 1), 5)
    mine = own_expert.astype(F32)

    def select(i):
        ys = source(i)
        small = sg[ys]
        grad, first, id0, id1 = small[0:4], small[4:8], small[8:12], small[12:16]
        is0, is1 = id0 == mine, id1 == mine
        named = jnp.where(is0 | is1, 1.0, 0.0)
        gate = jnp.where(is0, first, 1.0 - first)
        rank = jnp.dot(
            jnp.concatenate([named, named], axis=0).astype(BF16), seg[...], preferred_element_type=F32
        )
        dl = []
        jt = iota((8, 256), 0).astype(F32)
        for l in range(SECTIONS):
            sel = jnp.where(jnp.broadcast_to(id0[l:l + 1], (8, 256)) == jt, 1.0, 0.0)
            sel = sel - jnp.where(jnp.broadcast_to(id1[l:l + 1], (8, 256)) == jt, 1.0, 0.0)
            dl.append(jnp.broadcast_to(grad[l:l + 1], (8, 256)) * sel)
        d_hi, d_mid = split2(jnp.concatenate(dl, axis=0))
        side = jnp.concatenate([d_hi, d_mid, d_hi, jnp.zeros_like(d_hi)], axis=0)
        tops = topb[ys].reshape(SIDE * TOK, quarter)
        places, gates = [], []
        for l in range(SECTIONS):
            hit = (
                (jnp.broadcast_to(named[l:l + 1], (96, 256)) > 0.5)
                & (jnp.broadcast_to(rank[l:l + 1], (96, 256)) == s96)
                & own_block
            )
            gates.append(jnp.sum(
                jnp.where(hit, jnp.broadcast_to(gate[l:l + 1], (96, 256)), 0.0), axis=1, keepdims=True
            ))
            places.append(jnp.where(hit, 1.0, 0.0).astype(BF16))
        place = jnp.concatenate(places, axis=0)
        lefts = contract(place, side, 1, 1)
        above = jnp.right_shift(iota((96, 128), 1) & 31, 3)
        left = jnp.concatenate(
            [jnp.where(above > l, lefts[96 * l:96 * (l + 1)], 0.0).astype(BF16) for l in range(SECTIONS)], axis=0
        )
        rows = jnp.dot(place, tops, preferred_element_type=F32)
        rows = rows + jnp.dot(left, wq[...], preferred_element_type=F32)
        for l in range(SECTIONS):
            xs[i, l] = (gates[l] * rows[96 * l:96 * (l + 1)]).astype(BF16)
        for n in (2, 3, 0, 1):
            x_copy(i, n).start()
        sc[c, ys, x] = xs[i, x]

    def to_partner(i):
        three = sc.at[c, source(i), pl.ds(0, 3)]
        copy(three, three, xx_s.at[0], xx_r.at[i], partner).wait_recv()
        core_copy(i).start()

    def accumulate(i):
        ys = source(i)
        wait_hidden(i)
        part = sc.at[1 - c, ys]
        copy(part, part, cc_s.at[0], cc_r.at[i], partner).wait_recv()
        rows = jnp.dot(perm[...], hz[:, ys].reshape(384, 512), preferred_element_type=F32).astype(BF16)
        for q in range(2):
            cols = slice(q * quarter, (q + 1) * quarter)
            acc[:, cols] += contract(rows, sc[q, ys].reshape(384, quarter), 0, 0)

    acc[...] = jnp.zeros_like(acc)

    def small_wait(i):
        copy(sg.at[source(i)], sg.at[source(i)], sy_s.at[i], sy_r.at[i], partner).wait_recv()

    def body(i, carry):
        @pl.when(i < 3)
        def _():
            forward_hidden(i)

        @pl.when((i >= 4) & (i < SIDE + 1))
        def _():
            forward_hidden(i - 1)

        @pl.when((i >= 3) & (i < SIDE) & (i % 2 == 1))
        def _():
            take_ring(i)

        @pl.when((i >= 3) & (i < SIDE - 1) & (i % 2 == 1))
        def _():
            take_ring(i + 1)

        @pl.when((i >= 1) & (i < SIDE))
        def _():
            small_wait(i)

        @pl.when(i < SIDE)
        def _():
            select(i)

        @pl.when(i < 2)
        def _():
            take_hidden(i + 1)

        @pl.when((i >= 3) & (i < SIDE))
        def _():
            take_hidden(i)

        @pl.when((i >= 1) & (i < SIDE + 1))
        def _():
            relay(i - 1)

        @pl.when((i >= 2) & (i < SIDE + 2))
        def _():
            to_partner(i - 2)

        @pl.when(i == 2)
        def _():
            router_second()

        @pl.when(i == 1)
        def _():
            cotangents()

        @pl.when(i >= 3)
        def _():
            accumulate(i - 3)

        return carry

    lax.fori_loop(0, SIDE + 3, body, 0)
    down_ref[...] = acc[...].astype(BF16)
    for k in range(1, SIDE):
        part = rzr.at[(z + SIDE - k) % SIDE]
        copy(part, part, rz_s.at[k - 1], rz_r.at[k - 1], partner).wait_recv()
    total = rzr[0]
    for k in range(1, SIDE):
        total = total + rzr[k]
    router_ref[...] = total

    for k in range(1, SECTIONS):
        w_copy(k).wait_send()
    for n in range(1, 2 * SECTIONS):
        p_copy(n).wait_send()
    for r in range(4):
        for cc in range(2):
            if r == 0:
                @pl.when(jnp.logical_not(local & (c == cc)))
                def _():
                    tz_copy(r, cc).wait_send()
            else:
                tz_copy(r, cc).wait_send()
    for k in range(1, SIDE):
        sz_copy(k).wait_send()
        sy_copy(k).wait_send()
        ry_copy(k).wait_send()
        rz_copy(k).wait_send()


    def drained(ref, sem):
        copy(ref, ref, sem.at[0], cc_r.at[0], partner).wait_send()

    drained(topb.at[pl.ds(0, SIDE - 1)], ring_s)
    drained(hy.at[pl.ds(0, SIDE - 1)], hy_s)
    drained(hy, hz_s)
    drained(hy.at[:, pl.ds(0, 3)], hf_s)
    drained(xs.at[:, pl.ds(0, 3)], xx_s)
    drained(rel, rr_s)
    drained(xs, cc_s)


def per_device(top_cotangent, layer_inputs, router_weight, expert_ids, expert_outputs, hidden):
    micro, tok, half = top_cotangent.shape
    tokens = micro * tok
    half_ff = hidden.shape[4]
    width = router_weight.shape[1]
    quarter = half // 2
    tile = half_ff // SIDE
    strip = half // SIDE // SIDE
    vmem = pl.BlockSpec(memory_space=pltpu.VMEM)
    dma = pltpu.SemaphoreType.DMA
    hidden_rows = MICRO * CAP
    scratch = [
        pltpu.VMEM((SECTIONS, EXPERTS, width), F32),
        pltpu.VMEM((SECTIONS, 2, 48, tokens), F32),
        pltpu.VMEM((16, tokens), F32),
        pltpu.VMEM((SIDE, 16, SIDE * TOK), F32),
        pltpu.VMEM((SIDE, 16, SIDE * TOK), F32),
        pltpu.VMEM((SIDE, EXPERTS, 256), F32),
        pltpu.VMEM((SIDE, EXPERTS, 256), F32),
        pltpu.VMEM((SIDE, EXPERTS, 128), F32),
        pltpu.VMEM((SIDE, EXPERTS, 128), F32),
        pltpu.VMEM((SIDE, SIDE, TOK, quarter), BF16),
        pltpu.VMEM((WINDOW * hidden_rows, 256), BF16),
        pltpu.VMEM((SIDE, 4, hidden_rows, tile), BF16),
        pltpu.VMEM((SIDE, 4, hidden_rows, tile), BF16),
        pltpu.VMEM((SIDE, SIDE, hidden_rows, tile), BF16),
        pltpu.VMEM((384, 384), BF16),
        pltpu.VMEM((256, 256), BF16),
        pltpu.VMEM((128, quarter), BF16),
        pltpu.VMEM((SIDE, SECTIONS, SIDE * CAP, quarter), BF16),
        pltpu.VMEM((SIDE, 2, SIDE * CAP // 2, quarter), BF16),
        pltpu.VMEM((2, SIDE, SECTIONS, SIDE * CAP, quarter), BF16),
        pltpu.VMEM((tile, half), F32),
        pltpu.VMEM((tokens, 2, half_ff), BF16),
        dma((1,)),
        dma((3,)), dma((3,)),
        dma((7,)), dma((7,)),
        dma((4, 2)), dma((SIDE,)),
        dma((1,)), dma((SIDE,)),
        dma((7,)), dma((7,)),
        dma((SIDE,)), dma((SIDE,)),
        dma((7,)), dma((7,)),
        dma((7,)), dma((7,)),
        dma((1,)), dma((SIDE,)),
        dma((1,)), dma((SIDE, 2)),
        dma((1,)),
        dma((1,)), dma((SIDE,)),
        dma((1,)), dma((SIDE, 2)),
        dma((1,)), dma((SIDE,)),
    ]
    cotangent, down, router = pl.pallas_call(
        kernel,
        out_shape=(
            jax.ShapeDtypeStruct((tokens, half), BF16),
            jax.ShapeDtypeStruct((tile, half), BF16),
            jax.ShapeDtypeStruct((EXPERTS, 128), F32),
        ),
        in_specs=[vmem] * 5 + [pl.BlockSpec(memory_space=pl.ANY)],
        out_specs=(vmem, vmem, vmem),
        scratch_shapes=scratch,
        compiler_params=pltpu.CompilerParams(
            collective_id=0, has_side_effects=True, vmem_limit_bytes=50 * 1024 * 1024
        ),
        cost_estimate=pl.CostEstimate(flops=8_000_000_000, bytes_accessed=8_000_000, transcendentals=0),
    )(
        top_cotangent,
        layer_inputs.reshape(tokens, half),
        router_weight[0].T,
        expert_ids[0].transpose(0, 2, 1).reshape(micro * 2, tok),
        expert_outputs.reshape(tokens, 2, half),
        hidden.reshape(tokens, 2, half_ff),
    )
    return (
        cotangent.reshape(1, micro, tok, half),
        down.reshape(1, 1, 1, tile, half),
        router[:, :strip].T.reshape(1, 1, strip, EXPERTS),
    )


def solution(mesh):
    in_specs = (
        P(None, "ed", "tp"),
        P("section", None, "ed", "tp"),
        P("section", None, None),
        P("section", None, "ed", None),
        P("section", None, "ed", None, "tp"),
        P("section", None, "ed", None, "tp"),
    )
    out_specs = (
        P("section", None, "ed", "tp"),
        P("section", "tp", "ed", None, None),
        P("section", "tp", "ed", None),
    )
    return jax.shard_map(
        per_device, mesh=mesh, in_specs=in_specs, out_specs=out_specs, check_vma=False
    )
```

```python
import jax
import jax.numpy as jnp
from jax import lax
from jax.experimental import pallas as pl
from jax.experimental.pallas import tpu as pltpu
from jax.sharding import PartitionSpec as P

CAP = 12
MICRO = 4
TOK = 32
SIDE = 8
SECTIONS = 4
EXPERTS = 8
WINDOW = 4
HIGHEST = lax.Precision.HIGHEST
F32 = jnp.float32
BF16 = jnp.bfloat16
MESH = pl.DeviceIdType.MESH


def iota(shape, dim):
    return lax.broadcasted_iota(jnp.int32, shape, dim)


def divided(x, by):
    return ((x.astype(F32) + 0.5) * (1.0 / by)).astype(jnp.int32)


def contract(a, b, da, db, precision=None):
    return lax.dot_general(a, b, (((da,), (db,)), ((), ())), precision=precision, preferred_element_type=F32)


def split2(x):
    hi = x.astype(BF16)
    return hi, (x - hi.astype(F32)).astype(BF16)


def split3(x):
    hi = x.astype(BF16)
    rest = x - hi.astype(F32)
    mid = rest.astype(BF16)
    return hi, mid, (rest - mid.astype(F32)).astype(BF16)


def by_parts(x, rows, dims):
    parts = jnp.concatenate([p.astype(F32) for p in split3(x)], axis=0).astype(BF16)
    got = contract(parts, rows, 1, dims)
    n = x.shape[0]
    return got[:n] + got[n:2 * n] + got[2 * n:]


def earlier(segment_log2):
    r, c = iota((256, 256), 0), iota((256, 256), 1)
    same = jnp.right_shift(r, segment_log2) == jnp.right_shift(c, segment_log2)
    return jnp.where(same & (r < c), 1.0, 0.0).astype(BF16)


def kernel(
    top_ref, x_ref, w_ref, ids_ref, eo_ref, hid_ref,
    cot_ref, down_ref, router_ref,
    wb, pr, sm, szr, sg, ry, ryr, rz, rzr, topb, pick, hs, hy, hz, perm, seg, wq, xs, rel, sc, acc, hv, tv, xv, ev, iv, in_sem,
    w_s, w_r, p_s, p_r, tz_s, tz_r, ring_s, ring_r, sz_s, sz_r, sy_s, sy_r, ry_s, ry_r, rz_s, rz_r,
    hy_s, hy_r, hz_s, hz_r, hf_s, xx_s, xx_r, rr_s, rr_r, cc_s, cc_r,
):
    x = lax.axis_index("section")
    ed = lax.axis_index("ed")
    c = lax.axis_index("tp")
    y = ed // SIDE
    z = ed % SIDE
    half = top_ref.shape[2]
    quarter = half // 2
    own_half = z % 2
    own_expert = y // 2

    def at_x(k):
        return ((x + k) % SECTIONS, ed, c)

    def at_y(k):
        return (x, ((y + k) % SIDE) * SIDE + z, c)

    def at_z(k):
        return (x, y * SIDE + (z + k) % SIDE, c)

    partner = (x, ed, 1 - c)

    def off(i):
        return ((i + 1) // 2) * (1 - 2 * (i % 2))

    def source(i):
        return (y + SIDE + off(i)) % SIDE

    def copy(src, dst, send, recv, device):
        return pltpu.make_async_remote_copy(
            src_ref=src, dst_ref=dst, send_sem=send, recv_sem=recv, device_id=device, device_id_type=MESH
        )

    barrier = pltpu.get_barrier_semaphore()

    def greet(device):
        pl.semaphore_signal(barrier, inc=1, device_id=device, device_id_type=MESH)

    greet(partner)
    for k in range(1, SECTIONS):
        for cc in range(2):
            greet(((x + k) % SECTIONS, ed, cc))
    for k in range(1, SIDE):
        greet(at_y(k))
        for cc in range(2):
            greet((x, y * SIDE + (z + k) % SIDE, cc))

    loads = [
        pltpu.make_async_copy(src, dst, in_sem.at[n])
        for n, (src, dst) in enumerate(
            ((ids_ref, iv), (hid_ref, hv), (w_ref, wb.at[x]), (top_ref, tv), (x_ref, xv), (eo_ref, ev))
        )
    ]
    for load in loads:
        load.start()

    loads[0].wait()
    ids = iv[...].astype(F32).astype(BF16)
    route = iota((8, 256), 1)
    spread = (jnp.right_shift(iota((TOK, 256), 1), 1) & (TOK - 1)) == iota((TOK, 256), 0)
    wide = jnp.dot(ids, jnp.where(spread, 1.0, 0.0).astype(BF16), preferred_element_type=F32)
    own_row = iota((8, 256), 0) == 2 * jnp.right_shift(route, 6) + (route & 1)
    ids_row = jnp.sum(jnp.where(own_row, wide, 0.0), axis=0, keepdims=True)
    spread = (iota((TOK, 128), 1) & (TOK - 1)) == iota((TOK, 128), 0)
    wide = jnp.dot(ids, jnp.where(spread, 1.0, 0.0).astype(BF16), preferred_element_type=F32)
    first_row = iota((8, 128), 0) - 2 * jnp.right_shift(iota((8, 128), 1), 5)
    ids_first = jnp.sum(jnp.where(first_row == 0, wide, 0.0), axis=0, keepdims=True)
    ids_second = jnp.sum(jnp.where(first_row == 1, wide, 0.0), axis=0, keepdims=True)
    named = (jnp.broadcast_to(ids_row, (8, 256)) == iota((8, 256), 0).astype(F32)).astype(F32)
    rank = jnp.dot(named.astype(BF16), earlier(6), preferred_element_type=F32)
    r48 = iota((48, 256), 0)
    m48 = divided(r48, CAP)
    s48 = (r48 - CAP * m48).astype(F32)
    own_micro = m48 == jnp.right_shift(iota((48, 256), 1), 6)
    for e in range(WINDOW):
        hit = (
            (jnp.broadcast_to(named[e:e + 1], (48, 256)) > 0.5)
            & (jnp.broadcast_to(rank[e:e + 1], (48, 256)) == s48)
            & own_micro
        )
        pick[e * 48:(e + 1) * 48, :] = jnp.where(hit, 1.0, 0.0).astype(BF16)

    pl.semaphore_wait(barrier, 1 + 2 * (SECTIONS - 1) + 3 * (SIDE - 1))

    def w_copy(k):
        return copy(w_ref, wb.at[x], w_s.at[k - 1], w_r.at[k - 1], at_x(k))

    for k in range(1, SECTIONS):
        w_copy(k).start()

    tilt = (z + c) % 2
    local = tilt == 0

    def tz_copy(r, cc):
        zd = (z + 2 * r + tilt) % SIDE
        return copy(
            top_ref.at[x, :, pl.ds(cc * quarter, quarter)], topb.at[y, z], tz_s.at[r, cc], tz_r.at[z],
            (x, y * SIDE + zd, cc),
        )

    for r in range(4):
        for cc in range(2):
            if r == 0:
                @pl.when(jnp.logical_not(local & (c == cc)))
                def _():
                    tz_copy(r, cc).start()
            else:
                tz_copy(r, cc).start()

    loads[3].wait()

    @pl.when(local)
    def _():
        topb[y, z] = tv[x, :, pl.ds(pl.multiple_of(c * quarter, 128), quarter)]

    def hidden_block(f, carry):
        cols = hv[:, :, pl.ds(pl.multiple_of(f * 512, 512), 512)].reshape(256, 512)
        got = jnp.dot(pick[...], cols, preferred_element_type=F32).astype(BF16)
        for e in range(WINDOW):
            hs[2 * e + f // 4, f % 4] = got[e * 48:(e + 1) * 48]
        return carry

    loads[1].wait()
    lax.fori_loop(0, 8, hidden_block, 0)

    def hy_copy(i):
        yd = (y + SIDE - off(i)) % SIDE
        return copy(hs.at[yd], hy.at[y], hy_s.at[0], hy_r.at[i], (x, yd * SIDE + z, c))

    def hy_start(i, carry):
        hy_copy(i).start()
        return carry

    def ring_copy(block, first, count, item, k):
        part = topb.at[block, pl.ds(first, count)]
        return copy(part, part, ring_s.at[0], ring_r.at[item], at_y(k))

    def tz_wait(zs, carry):
        @pl.when(jnp.logical_not(local & (zs == z)))
        def _():
            copy(topb.at[y, zs], topb.at[y, zs], tz_s.at[0, 0], tz_r.at[zs], partner).wait_recv()
        return carry

    lax.fori_loop(0, SIDE, tz_wait, 0)
    ring_copy(y, 0, SIDE, 1, 1).start()
    ring_copy(y, 0, SIDE, 2, SIDE - 1).start()
    lax.fori_loop(1, 3, hy_start, 0)
    hy[y] = hs[y]

    pair = z // 2
    parity = z % 2

    def hz_copy(i, d):
        ys = source(i)
        if d == 0:
            target, j = z + 1 - 2 * parity, 1
        elif d == 1:
            target, j = 2 * ((pair + 1) % 4), 0
        elif d == 2:
            target, j = 2 * ((pair + 2) % 4) + 1 - parity, 0
        else:
            target, j = 2 * ((pair + 3) % 4) + 1, 0
        return copy(
            hy.at[ys, (pair + d) % 4], hz.at[z, ys], hz_s.at[0], hz_r.at[i, j], (x, y * SIDE + target, c)
        )

    def send_hidden(i):
        ys = source(i)
        for d in (2, 1, 3, 0):
            hz_copy(i, d).start()
        hz[z, ys] = hy[ys, pair]

    near = 2 * ((pair + 3 + 2 * parity) % 4)
    far = 2 * ((pair + 2) % 4) + 1 - parity
    other = (x, y * SIDE + z + 1 - 2 * parity, c)

    def forward_hidden(i):
        ys = source(i)
        three = hz.at[pl.ds(0, 3), ys]
        copy(three, three, hz_s.at[0], hz_r.at[i, 0], partner).wait_recv()
        two, one = hz.at[pl.ds(near, 2), ys], hz.at[far, ys]
        copy(two, two, hf_s.at[0], hz_r.at[i, 1], other).start()
        copy(one, one, hf_s.at[0], hz_r.at[i, 1], other).start()

    def wait_hidden(i):
        four = hz.at[pl.ds(0, 4), source(i)]
        copy(four, four, hz_s.at[0], hz_r.at[i, 1], partner).wait_recv()

    send_hidden(0)

    core_cols = pl.ds(pl.multiple_of(c * half, 128), half)
    for load in (loads[2], loads[4], loads[5]):
        load.wait()
    inputs = xv[...]
    top_tokens = tv[...].reshape(MICRO * TOK, half)
    outs = ev[...].reshape(256, half)
    r128, c256 = iota((128, 256), 0), iota((128, 256), 1)
    pairs = jnp.where(c256 == 2 * r128, 1.0, jnp.where(c256 == 2 * r128 + 1, -1.0, 0.0))
    pr[x, c, 0:8] = by_parts(wb[x, :, core_cols], inputs, 1)
    products = contract(top_tokens, outs, 1, 1)
    dots = jnp.sum(products * jnp.abs(pairs), axis=0, keepdims=True)
    dots = contract(jnp.broadcast_to(dots, (8, 256)), pairs, 1, 1, HIGHEST)
    lines = iota((8, 128), 0)
    pr[x, c, 8:16] = jnp.where(lines == 1, ids_first, jnp.where(lines == 2, ids_second, dots))

    def w_wait(k):
        copy(w_ref, wb.at[(x + SECTIONS - k) % SECTIONS], w_s.at[k - 1], w_r.at[k - 1], at_x(k)).wait_recv()

    for k in range(1, SECTIONS):
        w_wait(k)
    weights_half = wb[:, :, core_cols]
    crossed = by_parts(weights_half.reshape(SECTIONS * EXPERTS, half), outs, 1)
    pr[x, c, 16:48] = contract(crossed, pairs, 1, 1, HIGHEST)

    def p_copy(n):
        dx, dc = n // 2, n % 2
        return copy(pr.at[x, c], pr.at[x, c], p_s.at[n - 1], p_r.at[n - 1], ((x + dx) % SECTIONS, ed, (c + dc) % 2))

    for n in range(1, 2 * SECTIONS):
        p_copy(n).start()

    seg[...] = earlier(5)
    rp, cp = iota((384, 384), 0), iota((384, 384), 1)
    qp = divided(rp, CAP)
    perm[...] = jnp.where(
        cp == (qp & 7) * 48 + jnp.right_shift(qp, 3) * CAP + rp - CAP * qp, 1.0, 0.0
    ).astype(BF16)
    w_quarter = wb[:, :, pl.ds(pl.multiple_of(own_half * half + c * quarter, 128), quarter)]
    w_hi, w_mid = split2(w_quarter.reshape(SECTIONS * EXPERTS, quarter))
    wq[0:32] = w_hi
    wq[32:64] = w_hi
    wq[64:96] = w_mid
    wq[96:128] = jnp.zeros((32, quarter), BF16)
    ry[...] = jnp.zeros_like(ry)
    rz[...] = jnp.zeros_like(rz)

    for n in range(1, 2 * SECTIONS):
        dx, dc = n // 2, n % 2
        part = pr.at[(x + SECTIONS - dx) % SECTIONS, (c + dc) % 2]
        copy(part, part, p_s.at[n - 1], p_r.at[n - 1], partner).wait_recv()

    j8 = iota((8, 128), 0).astype(F32)
    firsts, grads, selects, dls = [], [None] * SECTIONS, [], [None] * SECTIONS
    for l in range(SECTIONS):
        logits = pr[l, 0, 0:8] + pr[l, 1, 0:8]
        id0, id1 = pr[l, 0, 9:10], pr[l, 0, 10:11]
        hot0 = jnp.where(jnp.broadcast_to(id0, (8, 128)) == j8, 1.0, 0.0)
        hot1 = jnp.where(jnp.broadcast_to(id1, (8, 128)) == j8, 1.0, 0.0)
        selects.append(hot0 - hot1)
        gap = jnp.sum(hot1 * logits, axis=0, keepdims=True) - jnp.sum(hot0 * logits, axis=0, keepdims=True)
        firsts.append(1.0 / (1.0 + jnp.exp(gap)))
        sm[4 + l:5 + l] = firsts[l]
        sm[8 + l:9 + l] = id0
        sm[12 + l:13 + l] = id1
    for l in range(SECTIONS - 1, -1, -1):
        total = pr[l, 0, 8:9] + pr[l, 1, 8:9]
        for a in range(l + 1, SECTIONS):
            cross = pr[l, 0, 16 + 8 * a:24 + 8 * a] + pr[l, 1, 16 + 8 * a:24 + 8 * a]
            total = total + grads[a] * jnp.sum(cross * selects[a], axis=0, keepdims=True)
        grads[l] = firsts[l] * (1.0 - firsts[l]) * total
        sm[l:l + 1] = grads[l]
        dls[l] = jnp.broadcast_to(grads[l], (8, 128)) * selects[l]

    to = iota((128, 256), 1) - z * TOK
    at = iota((128, 256), 0) - x * TOK
    put = jnp.where((to == at) & (to >= 0) & (to < TOK), 1.0, 0.0)
    szr[z] = jnp.dot(sm[...], put, precision=HIGHEST, preferred_element_type=F32)

    def sz_copy(k):
        return copy(szr.at[z], szr.at[z], sz_s.at[k - 1], sz_r.at[k - 1], at_z(k))

    for k in range(1, SIDE):
        sz_copy(k).start()

    def take_ring(i):
        part = topb.at[source(i)]
        copy(part, part, ring_s.at[0], ring_r.at[i], partner).wait_recv()

        @pl.when(i < 5)
        def _():
            ring_copy(source(i), 0, SIDE, i + 2, 1 + (1 - i % 2) * (SIDE - 2)).start()

        @pl.when(i == 5)
        def _():
            ring_copy(source(i), 0, 4, SIDE - 1, 1).start()

        @pl.when(i == 6)
        def _():
            ring_copy(source(i), 4, 4, SIDE - 1, SIDE - 1).start()

        @pl.when(i < 5)
        def _():
            hy_copy(i + 2).start()

        @pl.when(i == 4)
        def _():
            hy_copy(SIDE - 1).start()

    own_dl = jnp.zeros((8, 128), F32)
    for l in range(SECTIONS):
        own_dl = jnp.where(x == l, dls[l], own_dl)
    router_part = by_parts(own_dl, inputs, 0)
    strip = half // SIDE
    for k in range(SIDE):
        ry[k, :, 0:strip] = router_part[:, k * strip:(k + 1) * strip]

    def ry_copy(k):
        yd = (y + k) % SIDE
        return copy(ry.at[yd], ryr.at[y], ry_s.at[k - 1], ry_r.at[k - 1], at_y(k))

    for k in range(1, SIDE):
        ry_copy(k).start()
    ryr[y] = ry[y]

    def first_rings(i, carry):
        take_ring(i)
        return carry

    lax.fori_loop(1, 3, first_rings, 0)


    for k in range(1, SIDE):
        part = szr.at[(z + SIDE - k) % SIDE]
        copy(part, part, sz_s.at[k - 1], sz_r.at[k - 1], partner).wait_recv()
    total = szr[0]
    for k in range(1, SIDE):
        total = total + szr[k]
    sg[y] = total

    def sy_copy(i):
        return copy(sg.at[y], sg.at[y], sy_s.at[i], sy_r.at[i], at_y(SIDE - off(i)))

    for i in range(1, SIDE):
        sy_copy(i).start()


    def rz_copy(k):
        zd = (z + k) % SIDE
        return copy(rz.at[zd], rzr.at[z], rz_s.at[k - 1], rz_r.at[k - 1], at_z(k))

    def router_second():
        for k in range(1, SIDE):
            part = ryr.at[(y + SIDE - k) % SIDE]
            copy(part, part, ry_s.at[k - 1], ry_r.at[k - 1], partner).wait_recv()
        total = ryr[0]
        for k in range(1, SIDE):
            total = total + ryr[k]
        piece = strip // SIDE
        for k in range(SIDE):
            rz[k, :, 0:piece] = total[:, k * piece:(k + 1) * piece]
        for k in range(1, SIDE):
            rz_copy(k).start()
        rzr[z] = rz[z]

    def cotangents():
        cotangent = top_tokens
        for l in range(SECTIONS - 1, -1, -1):
            d_hi, d_mid, _ = split3(dls[l])
            w_hi, w_mid, _ = split3(wb[l, :, core_cols])
            left = jnp.concatenate([d.astype(F32) for d in (d_hi, d_mid, d_hi)], axis=0).astype(BF16)
            right = jnp.concatenate([w.astype(F32) for w in (w_hi, w_hi, w_mid)], axis=0).astype(BF16)
            step = contract(left, right, 0, 0)
            cotangent = jnp.where(l >= x, (cotangent.astype(F32) + step).astype(BF16), cotangent)
        cot_ref[...] = cotangent

    def take_hidden(i):
        copy(hs.at[0], hy.at[source(i)], hy_s.at[0], hy_r.at[i], partner).wait_recv()
        send_hidden(i)

    def x_copy(i, n):
        ys = source(i)
        if n < 2:
            k = 1 + 2 * n
            return copy(
                xs.at[i, (x + k) % SECTIONS], sc.at[c, ys, x], xx_s.at[0], xx_r.at[i], at_x(k)
            )
        n -= 2
        return copy(
            xs.at[i, (x + 2) % SECTIONS, pl.ds(48 * n, 48)], rel.at[i, n], xx_s.at[0], rr_r.at[i, n],
            at_x(1 + 2 * n),
        )

    def relay_copy(i, n):
        k = 1 + 2 * n
        return copy(
            rel.at[i, n], sc.at[c, source(i), (x + SECTIONS - k) % SECTIONS, pl.ds(48 * n, 48)],
            rr_s.at[0], xx_r.at[i], at_x(k),
        )

    def relay(i):
        for n in range(2):
            copy(rel.at[i, n], rel.at[i, n], rr_s.at[0], rr_r.at[i, n], partner).wait_recv()
            relay_copy(i, n).start()

    def core_copy(i):
        part = sc.at[c, source(i)]
        return copy(part, part, cc_s.at[0], cc_r.at[i], partner)

    r96 = iota((96, 256), 0)
    z96 = divided(r96, CAP)
    s96 = (r96 - CAP * z96).astype(F32)
    own_block = z96 == jnp.right_shift(iota((96, 256), 1), 5)
    mine = own_expert.astype(F32)

    def select(i):
        ys = source(i)
        small = sg[ys]
        grad, first, id0, id1 = small[0:4], small[4:8], small[8:12], small[12:16]
        is0, is1 = id0 == mine, id1 == mine
        named = jnp.where(is0 | is1, 1.0, 0.0)
        gate = jnp.where(is0, first, 1.0 - first)
        rank = jnp.dot(
            jnp.concatenate([named, named], axis=0).astype(BF16), seg[...], preferred_element_type=F32
        )
        dl = []
        jt = iota((8, 256), 0).astype(F32)
        for l in range(SECTIONS):
            sel = jnp.where(jnp.broadcast_to(id0[l:l + 1], (8, 256)) == jt, 1.0, 0.0)
            sel = sel - jnp.where(jnp.broadcast_to(id1[l:l + 1], (8, 256)) == jt, 1.0, 0.0)
            dl.append(jnp.broadcast_to(grad[l:l + 1], (8, 256)) * sel)
        d_hi, d_mid = split2(jnp.concatenate(dl, axis=0))
        side = jnp.concatenate([d_hi, d_mid, d_hi, jnp.zeros_like(d_hi)], axis=0)
        tops = topb[ys].reshape(SIDE * TOK, quarter)
        places, gates = [], []
        for l in range(SECTIONS):
            hit = (
                (jnp.broadcast_to(named[l:l + 1], (96, 256)) > 0.5)
                & (jnp.broadcast_to(rank[l:l + 1], (96, 256)) == s96)
                & own_block
            )
            gates.append(jnp.sum(
                jnp.where(hit, jnp.broadcast_to(gate[l:l + 1], (96, 256)), 0.0), axis=1, keepdims=True
            ))
            places.append(jnp.where(hit, 1.0, 0.0).astype(BF16))
        place = jnp.concatenate(places, axis=0)
        lefts = contract(place, side, 1, 1)
        above = jnp.right_shift(iota((96, 128), 1) & 31, 3)
        left = jnp.concatenate(
            [jnp.where(above > l, lefts[96 * l:96 * (l + 1)], 0.0).astype(BF16) for l in range(SECTIONS)], axis=0
        )
        rows = jnp.dot(place, tops, preferred_element_type=F32)
        rows = rows + jnp.dot(left, wq[...], preferred_element_type=F32)
        for l in range(SECTIONS):
            xs[i, l] = (gates[l] * rows[96 * l:96 * (l + 1)]).astype(BF16)
        for n in (2, 3, 0, 1):
            x_copy(i, n).start()
        sc[c, ys, x] = xs[i, x]

    def to_partner(i):
        three = sc.at[c, source(i), pl.ds(0, 3)]
        copy(three, three, xx_s.at[0], xx_r.at[i], partner).wait_recv()
        core_copy(i).start()

    def accumulate(i):
        ys = source(i)
        wait_hidden(i)
        part = sc.at[1 - c, ys]
        copy(part, part, cc_s.at[0], cc_r.at[i], partner).wait_recv()
        rows = jnp.dot(perm[...], hz[:, ys].reshape(384, 512), preferred_element_type=F32).astype(BF16)
        for q in range(2):
            cols = slice(q * quarter, (q + 1) * quarter)
            acc[:, cols] += contract(rows, sc[q, ys].reshape(384, quarter), 0, 0)

    acc[...] = jnp.zeros_like(acc)

    def small_wait(i):
        copy(sg.at[source(i)], sg.at[source(i)], sy_s.at[i], sy_r.at[i], partner).wait_recv()

    def body(i, carry):
        @pl.when(i < 3)
        def _():
            forward_hidden(i)

        @pl.when((i >= 4) & (i < SIDE + 1))
        def _():
            forward_hidden(i - 1)

        @pl.when((i >= 3) & (i < SIDE) & (i % 2 == 1))
        def _():
            take_ring(i)

        @pl.when((i >= 3) & (i < SIDE - 1) & (i % 2 == 1))
        def _():
            take_ring(i + 1)

        @pl.when((i >= 1) & (i < SIDE))
        def _():
            small_wait(i)

        @pl.when((i >= 1) & (i < SIDE))
        def _():
            select(i)

        @pl.when(i < 2)
        def _():
            take_hidden(i + 1)

        @pl.when((i >= 3) & (i < SIDE))
        def _():
            take_hidden(i)

        @pl.when((i >= 1) & (i < SIDE + 1))
        def _():
            relay(i - 1)

        @pl.when((i >= 2) & (i < SIDE + 2))
        def _():
            to_partner(i - 2)

        @pl.when(i == 2)
        def _():
            router_second()

        @pl.when(i == 1)
        def _():
            cotangents()

        @pl.when(i >= 3)
        def _():
            accumulate(i - 3)

        return carry

    select(0)
    lax.fori_loop(0, SIDE + 3, body, 0)
    down_ref[...] = acc[...].astype(BF16)
    for k in range(1, SIDE):
        part = rzr.at[(z + SIDE - k) % SIDE]
        copy(part, part, rz_s.at[k - 1], rz_r.at[k - 1], partner).wait_recv()
    total = rzr[0]
    for k in range(1, SIDE):
        total = total + rzr[k]
    router_ref[...] = total

    for k in range(1, SECTIONS):
        w_copy(k).wait_send()
    for n in range(1, 2 * SECTIONS):
        p_copy(n).wait_send()
    for r in range(4):
        for cc in range(2):
            if r == 0:
                @pl.when(jnp.logical_not(local & (c == cc)))
                def _():
                    tz_copy(r, cc).wait_send()
            else:
                tz_copy(r, cc).wait_send()
    for k in range(1, SIDE):
        sz_copy(k).wait_send()
        sy_copy(k).wait_send()
        ry_copy(k).wait_send()
        rz_copy(k).wait_send()


    def drained(ref, sem):
        copy(ref, ref, sem.at[0], cc_r.at[0], partner).wait_send()

    drained(topb.at[pl.ds(0, SIDE - 1)], ring_s)
    drained(hy.at[pl.ds(0, SIDE - 1)], hy_s)
    drained(hy, hz_s)
    drained(hy.at[:, pl.ds(0, 3)], hf_s)
    drained(xs.at[:, pl.ds(0, 3)], xx_s)
    drained(rel, rr_s)
    drained(xs, cc_s)


def per_device(top_cotangent, layer_inputs, router_weight, expert_ids, expert_outputs, hidden):
    micro, tok, half = top_cotangent.shape
    tokens = micro * tok
    half_ff = hidden.shape[4]
    width = router_weight.shape[1]
    quarter = half // 2
    tile = half_ff // SIDE
    strip = half // SIDE // SIDE
    vmem = pl.BlockSpec(memory_space=pltpu.VMEM)
    dma = pltpu.SemaphoreType.DMA
    hidden_rows = MICRO * CAP
    scratch = [
        pltpu.VMEM((SECTIONS, EXPERTS, width), F32),
        pltpu.VMEM((SECTIONS, 2, 48, tokens), F32),
        pltpu.VMEM((16, tokens), F32),
        pltpu.VMEM((SIDE, 16, SIDE * TOK), F32),
        pltpu.VMEM((SIDE, 16, SIDE * TOK), F32),
        pltpu.VMEM((SIDE, EXPERTS, 256), F32),
        pltpu.VMEM((SIDE, EXPERTS, 256), F32),
        pltpu.VMEM((SIDE, EXPERTS, 128), F32),
        pltpu.VMEM((SIDE, EXPERTS, 128), F32),
        pltpu.VMEM((SIDE, SIDE, TOK, quarter), BF16),
        pltpu.VMEM((WINDOW * hidden_rows, 256), BF16),
        pltpu.VMEM((SIDE, 4, hidden_rows, tile), BF16),
        pltpu.VMEM((SIDE, 4, hidden_rows, tile), BF16),
        pltpu.VMEM((SIDE, SIDE, hidden_rows, tile), BF16),
        pltpu.VMEM((384, 384), BF16),
        pltpu.VMEM((256, 256), BF16),
        pltpu.VMEM((128, quarter), BF16),
        pltpu.VMEM((SIDE, SECTIONS, SIDE * CAP, quarter), BF16),
        pltpu.VMEM((SIDE, 2, SIDE * CAP // 2, quarter), BF16),
        pltpu.VMEM((2, SIDE, SECTIONS, SIDE * CAP, quarter), BF16),
        pltpu.VMEM((tile, half), F32),
        pltpu.VMEM((tokens, 2, half_ff), BF16),
        pltpu.VMEM((micro, tok, half), BF16),
        pltpu.VMEM((tokens, half), BF16),
        pltpu.VMEM((tokens, 2, half), BF16),
        pltpu.VMEM((2 * micro, tok), jnp.int32),
        dma((6,)),
        dma((3,)), dma((3,)),
        dma((7,)), dma((7,)),
        dma((4, 2)), dma((SIDE,)),
        dma((1,)), dma((SIDE,)),
        dma((7,)), dma((7,)),
        dma((SIDE,)), dma((SIDE,)),
        dma((7,)), dma((7,)),
        dma((7,)), dma((7,)),
        dma((1,)), dma((SIDE,)),
        dma((1,)), dma((SIDE, 2)),
        dma((1,)),
        dma((1,)), dma((SIDE,)),
        dma((1,)), dma((SIDE, 2)),
        dma((1,)), dma((SIDE,)),
    ]
    cotangent, down, router = pl.pallas_call(
        kernel,
        out_shape=(
            jax.ShapeDtypeStruct((tokens, half), BF16),
            jax.ShapeDtypeStruct((tile, half), BF16),
            jax.ShapeDtypeStruct((EXPERTS, 128), F32),
        ),
        in_specs=[pl.BlockSpec(memory_space=pl.ANY)] * 6,
        out_specs=(vmem, vmem, vmem),
        scratch_shapes=scratch,
        compiler_params=pltpu.CompilerParams(
            collective_id=0, has_side_effects=True, vmem_limit_bytes=58 * 1024 * 1024
        ),
        cost_estimate=pl.CostEstimate(flops=8_000_000_000, bytes_accessed=8_000_000, transcendentals=0),
    )(
        top_cotangent,
        layer_inputs.reshape(tokens, half),
        router_weight[0].T,
        expert_ids[0].transpose(0, 2, 1).reshape(micro * 2, tok),
        expert_outputs.reshape(tokens, 2, half),
        hidden.reshape(tokens, 2, half_ff),
    )
    return (
        cotangent.reshape(1, micro, tok, half),
        down.reshape(1, 1, 1, tile, half),
        router[:, :strip].T.reshape(1, 1, strip, EXPERTS),
    )


def solution(mesh):
    in_specs = (
        P(None, "ed", "tp"),
        P("section", None, "ed", "tp"),
        P("section", None, None),
        P("section", None, "ed", None),
        P("section", None, "ed", None, "tp"),
        P("section", None, "ed", None, "tp"),
    )
    out_specs = (
        P("section", None, "ed", "tp"),
        P("section", "tp", "ed", None, None),
        P("section", "tp", "ed", None),
    )
    return jax.shard_map(
        per_device, mesh=mesh, in_specs=in_specs, out_specs=out_specs, check_vma=False
    )
```

```python
import jax
import jax.numpy as jnp
from jax import lax
from jax.experimental import pallas as pl
from jax.experimental.pallas import tpu as pltpu
from jax.sharding import PartitionSpec as P

CAP = 12
MICRO = 4
TOK = 32
SIDE = 8
SECTIONS = 4
EXPERTS = 8
WINDOW = 4
HIGHEST = lax.Precision.HIGHEST
F32 = jnp.float32
BF16 = jnp.bfloat16
MESH = pl.DeviceIdType.MESH


def iota(shape, dim):
    return lax.broadcasted_iota(jnp.int32, shape, dim)


def divided(x, by):
    return ((x.astype(F32) + 0.5) * (1.0 / by)).astype(jnp.int32)


def contract(a, b, da, db, precision=None):
    return lax.dot_general(a, b, (((da,), (db,)), ((), ())), precision=precision, preferred_element_type=F32)


def split2(x):
    hi = x.astype(BF16)
    return hi, (x - hi.astype(F32)).astype(BF16)


def split3(x):
    hi = x.astype(BF16)
    rest = x - hi.astype(F32)
    mid = rest.astype(BF16)
    return hi, mid, (rest - mid.astype(F32)).astype(BF16)


def by_parts(x, rows, dims):
    parts = jnp.concatenate([p.astype(F32) for p in split3(x)], axis=0).astype(BF16)
    got = contract(parts, rows, 1, dims)
    n = x.shape[0]
    return got[:n] + got[n:2 * n] + got[2 * n:]


def earlier(segment_log2):
    r, c = iota((256, 256), 0), iota((256, 256), 1)
    same = jnp.right_shift(r, segment_log2) == jnp.right_shift(c, segment_log2)
    return jnp.where(same & (r < c), 1.0, 0.0).astype(BF16)


def kernel(
    top_ref, x_ref, w_ref, ids_ref, eo_ref, hid_ref,
    cot_ref, down_ref, router_ref,
    wb, pr, sm, szr, sg, ry, ryr, rz, rzr, topb, pick, hs, hy, hz, perm, seg, wq, xs, rel, sc, acc, hv, hv_sem,
    w_s, w_r, p_s, p_r, tz_s, tz_r, ring_s, ring_r, sz_s, sz_r, sy_s, sy_r, ry_s, ry_r, rz_s, rz_r,
    hy_s, hy_r, hz_s, hz_r, hf_s, xx_s, xx_r, rr_s, rr_r, cc_s, cc_r,
):
    x = lax.axis_index("section")
    ed = lax.axis_index("ed")
    c = lax.axis_index("tp")
    y = ed // SIDE
    z = ed % SIDE
    half = top_ref.shape[2]
    quarter = half // 2
    own_half = z % 2
    own_expert = y // 2

    def at_x(k):
        return ((x + k) % SECTIONS, ed, c)

    def at_y(k):
        return (x, ((y + k) % SIDE) * SIDE + z, c)

    def at_z(k):
        return (x, y * SIDE + (z + k) % SIDE, c)

    partner = (x, ed, 1 - c)

    def off(i):
        return ((i + 1) // 2) * (1 - 2 * (i % 2))

    def source(i):
        return (y + SIDE + off(i)) % SIDE

    def copy(src, dst, send, recv, device):
        return pltpu.make_async_remote_copy(
            src_ref=src, dst_ref=dst, send_sem=send, recv_sem=recv, device_id=device, device_id_type=MESH
        )

    barrier = pltpu.get_barrier_semaphore()

    def greet(device):
        pl.semaphore_signal(barrier, inc=1, device_id=device, device_id_type=MESH)

    greet(partner)
    for k in range(1, SECTIONS):
        for cc in range(2):
            greet(((x + k) % SECTIONS, ed, cc))
    for k in range(1, SIDE):
        greet(at_y(k))
        for cc in range(2):
            greet((x, y * SIDE + (z + k) % SIDE, cc))

    load = pltpu.make_async_copy(hid_ref, hv, hv_sem.at[0])
    load.start()

    ids = ids_ref[...].astype(F32).astype(BF16)
    route = iota((8, 256), 1)
    spread = (jnp.right_shift(iota((TOK, 256), 1), 1) & (TOK - 1)) == iota((TOK, 256), 0)
    wide = jnp.dot(ids, jnp.where(spread, 1.0, 0.0).astype(BF16), preferred_element_type=F32)
    own_row = iota((8, 256), 0) == 2 * jnp.right_shift(route, 6) + (route & 1)
    ids_row = jnp.sum(jnp.where(own_row, wide, 0.0), axis=0, keepdims=True)
    spread = (iota((TOK, 128), 1) & (TOK - 1)) == iota((TOK, 128), 0)
    wide = jnp.dot(ids, jnp.where(spread, 1.0, 0.0).astype(BF16), preferred_element_type=F32)
    first_row = iota((8, 128), 0) - 2 * jnp.right_shift(iota((8, 128), 1), 5)
    ids_first = jnp.sum(jnp.where(first_row == 0, wide, 0.0), axis=0, keepdims=True)
    ids_second = jnp.sum(jnp.where(first_row == 1, wide, 0.0), axis=0, keepdims=True)
    named = (jnp.broadcast_to(ids_row, (8, 256)) == iota((8, 256), 0).astype(F32)).astype(F32)
    rank = jnp.dot(named.astype(BF16), earlier(6), preferred_element_type=F32)
    r48 = iota((48, 256), 0)
    m48 = divided(r48, CAP)
    s48 = (r48 - CAP * m48).astype(F32)
    own_micro = m48 == jnp.right_shift(iota((48, 256), 1), 6)
    for e in range(WINDOW):
        hit = (
            (jnp.broadcast_to(named[e:e + 1], (48, 256)) > 0.5)
            & (jnp.broadcast_to(rank[e:e + 1], (48, 256)) == s48)
            & own_micro
        )
        pick[e * 48:(e + 1) * 48, :] = jnp.where(hit, 1.0, 0.0).astype(BF16)

    pl.semaphore_wait(barrier, 1 + 2 * (SECTIONS - 1) + 3 * (SIDE - 1))

    def w_copy(k):
        return copy(w_ref, wb.at[x], w_s.at[k - 1], w_r.at[k - 1], at_x(k))

    for k in range(1, SECTIONS):
        w_copy(k).start()
    wb[x] = w_ref[...]

    tilt = (z + c) % 2
    local = tilt == 0

    def tz_copy(r, cc):
        zd = (z + 2 * r + tilt) % SIDE
        return copy(
            top_ref.at[x, :, pl.ds(cc * quarter, quarter)], topb.at[y, z], tz_s.at[r, cc], tz_r.at[z],
            (x, y * SIDE + zd, cc),
        )

    for r in range(4):
        for cc in range(2):
            if r == 0:
                @pl.when(jnp.logical_not(local & (c == cc)))
                def _():
                    tz_copy(r, cc).start()
            else:
                tz_copy(r, cc).start()

    @pl.when(local)
    def _():
        topb[y, z] = top_ref[x, :, pl.ds(pl.multiple_of(c * quarter, 128), quarter)]

    def hidden_block(f, carry):
        cols = hv[:, :, pl.ds(pl.multiple_of(f * 512, 512), 512)].reshape(256, 512)
        got = jnp.dot(pick[...], cols, preferred_element_type=F32).astype(BF16)
        for e in range(WINDOW):
            hs[2 * e + f // 4, f % 4] = got[e * 48:(e + 1) * 48]
        return carry

    load.wait()
    lax.fori_loop(0, 8, hidden_block, 0)

    def hy_copy(i):
        yd = (y + SIDE - off(i)) % SIDE
        return copy(hs.at[yd], hy.at[y], hy_s.at[0], hy_r.at[i], (x, yd * SIDE + z, c))

    def hy_start(i, carry):
        hy_copy(i).start()
        return carry

    def ring_copy(block, first, count, item, k):
        part = topb.at[block, pl.ds(first, count)]
        return copy(part, part, ring_s.at[0], ring_r.at[item], at_y(k))

    def tz_wait(zs, carry):
        @pl.when(jnp.logical_not(local & (zs == z)))
        def _():
            copy(topb.at[y, zs], topb.at[y, zs], tz_s.at[0, 0], tz_r.at[zs], partner).wait_recv()
        return carry

    lax.fori_loop(0, SIDE, tz_wait, 0)
    ring_copy(y, 0, SIDE, 1, 1).start()
    ring_copy(y, 0, SIDE, 2, SIDE - 1).start()
    lax.fori_loop(1, SIDE, hy_start, 0)
    hy[y] = hs[y]

    pair = z // 2
    parity = z % 2

    def hz_copy(i, d):
        ys = source(i)
        if d == 0:
            target, j = z + 1 - 2 * parity, 1
        elif d == 1:
            target, j = 2 * ((pair + 1) % 4), 0
        elif d == 2:
            target, j = 2 * ((pair + 2) % 4) + 1 - parity, 0
        else:
            target, j = 2 * ((pair + 3) % 4) + 1, 0
        return copy(
            hy.at[ys, (pair + d) % 4], hz.at[z, ys], hz_s.at[0], hz_r.at[i, j], (x, y * SIDE + target, c)
        )

    def send_hidden(i):
        ys = source(i)
        for d in (2, 1, 3, 0):
            hz_copy(i, d).start()
        hz[z, ys] = hy[ys, pair]

    near = 2 * ((pair + 3 + 2 * parity) % 4)
    far = 2 * ((pair + 2) % 4) + 1 - parity
    other = (x, y * SIDE + z + 1 - 2 * parity, c)

    def forward_hidden(i):
        ys = source(i)
        three = hz.at[pl.ds(0, 3), ys]
        copy(three, three, hz_s.at[0], hz_r.at[i, 0], partner).wait_recv()
        two, one = hz.at[pl.ds(near, 2), ys], hz.at[far, ys]
        copy(two, two, hf_s.at[0], hz_r.at[i, 1], other).start()
        copy(one, one, hf_s.at[0], hz_r.at[i, 1], other).start()

    def wait_hidden(i):
        four = hz.at[pl.ds(0, 4), source(i)]
        copy(four, four, hz_s.at[0], hz_r.at[i, 1], partner).wait_recv()

    send_hidden(0)

    core_cols = pl.ds(pl.multiple_of(c * half, 128), half)
    inputs = x_ref[...]
    top_tokens = top_ref[...].reshape(MICRO * TOK, half)
    outs = eo_ref[...].reshape(256, half)
    r128, c256 = iota((128, 256), 0), iota((128, 256), 1)
    pairs = jnp.where(c256 == 2 * r128, 1.0, jnp.where(c256 == 2 * r128 + 1, -1.0, 0.0))
    pr[x, c, 0:8] = by_parts(w_ref[:, core_cols], inputs, 1)
    products = contract(top_tokens, outs, 1, 1)
    dots = jnp.sum(products * jnp.abs(pairs), axis=0, keepdims=True)
    dots = contract(jnp.broadcast_to(dots, (8, 256)), pairs, 1, 1, HIGHEST)
    lines = iota((8, 128), 0)
    pr[x, c, 8:16] = jnp.where(lines == 1, ids_first, jnp.where(lines == 2, ids_second, dots))

    def w_wait(k):
        copy(w_ref, wb.at[(x + SECTIONS - k) % SECTIONS], w_s.at[k - 1], w_r.at[k - 1], at_x(k)).wait_recv()

    for k in range(1, SECTIONS):
        w_wait(k)
    weights_half = wb[:, :, core_cols]
    crossed = by_parts(weights_half.reshape(SECTIONS * EXPERTS, half), outs, 1)
    pr[x, c, 16:48] = contract(crossed, pairs, 1, 1, HIGHEST)

    def p_copy(n):
        dx, dc = n // 2, n % 2
        return copy(pr.at[x, c], pr.at[x, c], p_s.at[n - 1], p_r.at[n - 1], ((x + dx) % SECTIONS, ed, (c + dc) % 2))

    for n in range(1, 2 * SECTIONS):
        p_copy(n).start()

    seg[...] = earlier(5)
    rp, cp = iota((384, 384), 0), iota((384, 384), 1)
    qp = divided(rp, CAP)
    perm[...] = jnp.where(
        cp == (qp & 7) * 48 + jnp.right_shift(qp, 3) * CAP + rp - CAP * qp, 1.0, 0.0
    ).astype(BF16)
    w_quarter = wb[:, :, pl.ds(pl.multiple_of(own_half * half + c * quarter, 128), quarter)]
    w_hi, w_mid = split2(w_quarter.reshape(SECTIONS * EXPERTS, quarter))
    wq[0:32] = w_hi
    wq[32:64] = w_hi
    wq[64:96] = w_mid
    wq[96:128] = jnp.zeros((32, quarter), BF16)
    ry[...] = jnp.zeros_like(ry)
    rz[...] = jnp.zeros_like(rz)

    for n in range(1, 2 * SECTIONS):
        dx, dc = n // 2, n % 2
        part = pr.at[(x + SECTIONS - dx) % SECTIONS, (c + dc) % 2]
        copy(part, part, p_s.at[n - 1], p_r.at[n - 1], partner).wait_recv()

    j8 = iota((8, 128), 0).astype(F32)
    firsts, grads, selects, dls = [], [None] * SECTIONS, [], [None] * SECTIONS
    for l in range(SECTIONS):
        logits = pr[l, 0, 0:8] + pr[l, 1, 0:8]
        id0, id1 = pr[l, 0, 9:10], pr[l, 0, 10:11]
        hot0 = jnp.where(jnp.broadcast_to(id0, (8, 128)) == j8, 1.0, 0.0)
        hot1 = jnp.where(jnp.broadcast_to(id1, (8, 128)) == j8, 1.0, 0.0)
        selects.append(hot0 - hot1)
        gap = jnp.sum(hot1 * logits, axis=0, keepdims=True) - jnp.sum(hot0 * logits, axis=0, keepdims=True)
        firsts.append(1.0 / (1.0 + jnp.exp(gap)))
        sm[4 + l:5 + l] = firsts[l]
        sm[8 + l:9 + l] = id0
        sm[12 + l:13 + l] = id1
    for l in range(SECTIONS - 1, -1, -1):
        total = pr[l, 0, 8:9] + pr[l, 1, 8:9]
        for a in range(l + 1, SECTIONS):
            cross = pr[l, 0, 16 + 8 * a:24 + 8 * a] + pr[l, 1, 16 + 8 * a:24 + 8 * a]
            total = total + grads[a] * jnp.sum(cross * selects[a], axis=0, keepdims=True)
        grads[l] = firsts[l] * (1.0 - firsts[l]) * total
        sm[l:l + 1] = grads[l]
        dls[l] = jnp.broadcast_to(grads[l], (8, 128)) * selects[l]

    to = iota((128, 256), 1) - z * TOK
    at = iota((128, 256), 0) - x * TOK
    put = jnp.where((to == at) & (to >= 0) & (to < TOK), 1.0, 0.0)
    szr[z] = jnp.dot(sm[...], put, precision=HIGHEST, preferred_element_type=F32)

    def sz_copy(k):
        return copy(szr.at[z], szr.at[z], sz_s.at[k - 1], sz_r.at[k - 1], at_z(k))

    for k in range(1, SIDE):
        sz_copy(k).start()

    def take_ring(i):
        part = topb.at[source(i)]
        copy(part, part, ring_s.at[0], ring_r.at[i], partner).wait_recv()

        @pl.when(i < 5)
        def _():
            ring_copy(source(i), 0, SIDE, i + 2, 1 + (1 - i % 2) * (SIDE - 2)).start()

        @pl.when(i == 5)
        def _():
            ring_copy(source(i), 0, 4, SIDE - 1, 1).start()

        @pl.when(i == 6)
        def _():
            ring_copy(source(i), 4, 4, SIDE - 1, SIDE - 1).start()

    own_dl = jnp.zeros((8, 128), F32)
    for l in range(SECTIONS):
        own_dl = jnp.where(x == l, dls[l], own_dl)
    router_part = by_parts(own_dl, inputs, 0)
    strip = half // SIDE
    for k in range(SIDE):
        ry[k, :, 0:strip] = router_part[:, k * strip:(k + 1) * strip]

    def ry_copy(k):
        yd = (y + k) % SIDE
        return copy(ry.at[yd], ryr.at[y], ry_s.at[k - 1], ry_r.at[k - 1], at_y(k))

    for k in range(1, SIDE):
        ry_copy(k).start()
    ryr[y] = ry[y]


    for k in range(1, SIDE):
        part = szr.at[(z + SIDE - k) % SIDE]
        copy(part, part, sz_s.at[k - 1], sz_r.at[k - 1], partner).wait_recv()
    total = szr[0]
    for k in range(1, SIDE):
        total = total + szr[k]
    sg[y] = total

    def sy_copy(i):
        return copy(sg.at[y], sg.at[y], sy_s.at[i], sy_r.at[i], at_y(SIDE - off(i)))

    for i in range(1, SIDE):
        sy_copy(i).start()

    def first_rings(i, carry):
        take_ring(i)
        return carry

    lax.fori_loop(1, 3, first_rings, 0)

    def rz_copy(k):
        zd = (z + k) % SIDE
        return copy(rz.at[zd], rzr.at[z], rz_s.at[k - 1], rz_r.at[k - 1], at_z(k))

    def router_second():
        for k in range(1, SIDE):
            part = ryr.at[(y + SIDE - k) % SIDE]
            copy(part, part, ry_s.at[k - 1], ry_r.at[k - 1], partner).wait_recv()
        total = ryr[0]
        for k in range(1, SIDE):
            total = total + ryr[k]
        piece = strip // SIDE
        for k in range(SIDE):
            rz[k, :, 0:piece] = total[:, k * piece:(k + 1) * piece]
        for k in range(1, SIDE):
            rz_copy(k).start()
        rzr[z] = rz[z]

    def cotangents():
        cotangent = top_tokens
        for l in range(SECTIONS - 1, -1, -1):
            d_hi, d_mid, _ = split3(dls[l])
            w_hi, w_mid, _ = split3(wb[l, :, core_cols])
            left = jnp.concatenate([d.astype(F32) for d in (d_hi, d_mid, d_hi)], axis=0).astype(BF16)
            right = jnp.concatenate([w.astype(F32) for w in (w_hi, w_hi, w_mid)], axis=0).astype(BF16)
            step = contract(left, right, 0, 0)
            cotangent = jnp.where(l >= x, (cotangent.astype(F32) + step).astype(BF16), cotangent)
        cot_ref[...] = cotangent

    def take_hidden(i):
        copy(hs.at[0], hy.at[source(i)], hy_s.at[0], hy_r.at[i], partner).wait_recv()
        send_hidden(i)

    def x_copy(i, n):
        ys = source(i)
        if n < 2:
            k = 1 + 2 * n
            return copy(
                xs.at[i, (x + k) % SECTIONS], sc.at[c, ys, x], xx_s.at[0], xx_r.at[i], at_x(k)
            )
        n -= 2
        return copy(
            xs.at[i, (x + 2) % SECTIONS, pl.ds(48 * n, 48)], rel.at[i, n], xx_s.at[0], rr_r.at[i, n],
            at_x(1 + 2 * n),
        )

    def relay_copy(i, n):
        k = 1 + 2 * n
        return copy(
            rel.at[i, n], sc.at[c, source(i), (x + SECTIONS - k) % SECTIONS, pl.ds(48 * n, 48)],
            rr_s.at[0], xx_r.at[i], at_x(k),
        )

    def relay(i):
        for n in range(2):
            copy(rel.at[i, n], rel.at[i, n], rr_s.at[0], rr_r.at[i, n], partner).wait_recv()
            relay_copy(i, n).start()

    def core_copy(i):
        part = sc.at[c, source(i)]
        return copy(part, part, cc_s.at[0], cc_r.at[i], partner)

    r96 = iota((96, 256), 0)
    z96 = divided(r96, CAP)
    s96 = (r96 - CAP * z96).astype(F32)
    own_block = z96 == jnp.right_shift(iota((96, 256), 1), 5)
    mine = own_expert.astype(F32)

    def select(i):
        ys = source(i)
        small = sg[ys]
        grad, first, id0, id1 = small[0:4], small[4:8], small[8:12], small[12:16]
        is0, is1 = id0 == mine, id1 == mine
        named = jnp.where(is0 | is1, 1.0, 0.0)
        gate = jnp.where(is0, first, 1.0 - first)
        rank = jnp.dot(
            jnp.concatenate([named, named], axis=0).astype(BF16), seg[...], preferred_element_type=F32
        )
        dl = []
        jt = iota((8, 256), 0).astype(F32)
        for l in range(SECTIONS):
            sel = jnp.where(jnp.broadcast_to(id0[l:l + 1], (8, 256)) == jt, 1.0, 0.0)
            sel = sel - jnp.where(jnp.broadcast_to(id1[l:l + 1], (8, 256)) == jt, 1.0, 0.0)
            dl.append(jnp.broadcast_to(grad[l:l + 1], (8, 256)) * sel)
        d_hi, d_mid = split2(jnp.concatenate(dl, axis=0))
        side = jnp.concatenate([d_hi, d_mid, d_hi, jnp.zeros_like(d_hi)], axis=0)
        tops = topb[ys].reshape(SIDE * TOK, quarter)
        places, gates = [], []
        for l in range(SECTIONS):
            hit = (
                (jnp.broadcast_to(named[l:l + 1], (96, 256)) > 0.5)
                & (jnp.broadcast_to(rank[l:l + 1], (96, 256)) == s96)
                & own_block
            )
            gates.append(jnp.sum(
                jnp.where(hit, jnp.broadcast_to(gate[l:l + 1], (96, 256)), 0.0), axis=1, keepdims=True
            ))
            places.append(jnp.where(hit, 1.0, 0.0).astype(BF16))
        place = jnp.concatenate(places, axis=0)
        lefts = contract(place, side, 1, 1)
        above = jnp.right_shift(iota((96, 128), 1) & 31, 3)
        left = jnp.concatenate(
            [jnp.where(above > l, lefts[96 * l:96 * (l + 1)], 0.0).astype(BF16) for l in range(SECTIONS)], axis=0
        )
        rows = jnp.dot(place, tops, preferred_element_type=F32)
        rows = rows + jnp.dot(left, wq[...], preferred_element_type=F32)
        for l in range(SECTIONS):
            xs[i, l] = (gates[l] * rows[96 * l:96 * (l + 1)]).astype(BF16)
        for n in (2, 3, 0, 1):
            x_copy(i, n).start()
        sc[c, ys, x] = xs[i, x]

    def to_partner(i):
        three = sc.at[c, source(i), pl.ds(0, 3)]
        copy(three, three, xx_s.at[0], xx_r.at[i], partner).wait_recv()
        core_copy(i).start()

    def accumulate(i):
        ys = source(i)
        wait_hidden(i)
        part = sc.at[1 - c, ys]
        copy(part, part, cc_s.at[0], cc_r.at[i], partner).wait_recv()
        rows = jnp.dot(perm[...], hz[:, ys].reshape(384, 512), preferred_element_type=F32).astype(BF16)
        for q in range(2):
            cols = slice(q * quarter, (q + 1) * quarter)
            acc[:, cols] += contract(rows, sc[q, ys].reshape(384, quarter), 0, 0)

    acc[...] = jnp.zeros_like(acc)

    def small_wait(i):
        copy(sg.at[source(i)], sg.at[source(i)], sy_s.at[i], sy_r.at[i], partner).wait_recv()

    def body(i, carry):
        @pl.when(i < 3)
        def _():
            forward_hidden(i)

        @pl.when((i >= 4) & (i < SIDE + 1))
        def _():
            forward_hidden(i - 1)

        @pl.when((i >= 3) & (i < SIDE) & (i % 2 == 1))
        def _():
            take_ring(i)

        @pl.when((i >= 3) & (i < SIDE - 1) & (i % 2 == 1))
        def _():
            take_ring(i + 1)

        @pl.when((i >= 1) & (i < SIDE))
        def _():
            small_wait(i)

        @pl.when(i < SIDE)
        def _():
            select(i)

        @pl.when(i < 2)
        def _():
            take_hidden(i + 1)

        @pl.when((i >= 3) & (i < SIDE))
        def _():
            take_hidden(i)

        @pl.when((i >= 1) & (i < SIDE + 1))
        def _():
            relay(i - 1)

        @pl.when((i >= 2) & (i < SIDE + 2))
        def _():
            to_partner(i - 2)

        @pl.when(i == 2)
        def _():
            router_second()

        @pl.when(i == 1)
        def _():
            cotangents()

        @pl.when(i >= 3)
        def _():
            accumulate(i - 3)

        return carry

    lax.fori_loop(0, SIDE + 3, body, 0)
    down_ref[...] = acc[...].astype(BF16)
    for k in range(1, SIDE):
        part = rzr.at[(z + SIDE - k) % SIDE]
        copy(part, part, rz_s.at[k - 1], rz_r.at[k - 1], partner).wait_recv()
    total = rzr[0]
    for k in range(1, SIDE):
        total = total + rzr[k]
    router_ref[...] = total

    for k in range(1, SECTIONS):
        w_copy(k).wait_send()
    for n in range(1, 2 * SECTIONS):
        p_copy(n).wait_send()
    for r in range(4):
        for cc in range(2):
            if r == 0:
                @pl.when(jnp.logical_not(local & (c == cc)))
                def _():
                    tz_copy(r, cc).wait_send()
            else:
                tz_copy(r, cc).wait_send()
    for k in range(1, SIDE):
        sz_copy(k).wait_send()
        sy_copy(k).wait_send()
        ry_copy(k).wait_send()
        rz_copy(k).wait_send()


    def drained(ref, sem):
        copy(ref, ref, sem.at[0], cc_r.at[0], partner).wait_send()

    drained(topb.at[pl.ds(0, SIDE - 1)], ring_s)
    drained(hy.at[pl.ds(0, SIDE - 1)], hy_s)
    drained(hy, hz_s)
    drained(hy.at[:, pl.ds(0, 3)], hf_s)
    drained(xs.at[:, pl.ds(0, 3)], xx_s)
    drained(rel, rr_s)
    drained(xs, cc_s)


def per_device(top_cotangent, layer_inputs, router_weight, expert_ids, expert_outputs, hidden):
    micro, tok, half = top_cotangent.shape
    tokens = micro * tok
    half_ff = hidden.shape[4]
    width = router_weight.shape[1]
    quarter = half // 2
    tile = half_ff // SIDE
    strip = half // SIDE // SIDE
    vmem = pl.BlockSpec(memory_space=pltpu.VMEM)
    dma = pltpu.SemaphoreType.DMA
    hidden_rows = MICRO * CAP
    scratch = [
        pltpu.VMEM((SECTIONS, EXPERTS, width), F32),
        pltpu.VMEM((SECTIONS, 2, 48, tokens), F32),
        pltpu.VMEM((16, tokens), F32),
        pltpu.VMEM((SIDE, 16, SIDE * TOK), F32),
        pltpu.VMEM((SIDE, 16, SIDE * TOK), F32),
        pltpu.VMEM((SIDE, EXPERTS, 256), F32),
        pltpu.VMEM((SIDE, EXPERTS, 256), F32),
        pltpu.VMEM((SIDE, EXPERTS, 128), F32),
        pltpu.VMEM((SIDE, EXPERTS, 128), F32),
        pltpu.VMEM((SIDE, SIDE, TOK, quarter), BF16),
        pltpu.VMEM((WINDOW * hidden_rows, 256), BF16),
        pltpu.VMEM((SIDE, 4, hidden_rows, tile), BF16),
        pltpu.VMEM((SIDE, 4, hidden_rows, tile), BF16),
        pltpu.VMEM((SIDE, SIDE, hidden_rows, tile), BF16),
        pltpu.VMEM((384, 384), BF16),
        pltpu.VMEM((256, 256), BF16),
        pltpu.VMEM((128, quarter), BF16),
        pltpu.VMEM((SIDE, SECTIONS, SIDE * CAP, quarter), BF16),
        pltpu.VMEM((SIDE, 2, SIDE * CAP // 2, quarter), BF16),
        pltpu.VMEM((2, SIDE, SECTIONS, SIDE * CAP, quarter), BF16),
        pltpu.VMEM((tile, half), F32),
        pltpu.VMEM((tokens, 2, half_ff), BF16),
        dma((1,)),
        dma((3,)), dma((3,)),
        dma((7,)), dma((7,)),
        dma((4, 2)), dma((SIDE,)),
        dma((1,)), dma((SIDE,)),
        dma((7,)), dma((7,)),
        dma((SIDE,)), dma((SIDE,)),
        dma((7,)), dma((7,)),
        dma((7,)), dma((7,)),
        dma((1,)), dma((SIDE,)),
        dma((1,)), dma((SIDE, 2)),
        dma((1,)),
        dma((1,)), dma((SIDE,)),
        dma((1,)), dma((SIDE, 2)),
        dma((1,)), dma((SIDE,)),
    ]
    cotangent, down, router = pl.pallas_call(
        kernel,
        out_shape=(
            jax.ShapeDtypeStruct((tokens, half), BF16),
            jax.ShapeDtypeStruct((tile, half), BF16),
            jax.ShapeDtypeStruct((EXPERTS, 128), F32),
        ),
        in_specs=[vmem] * 5 + [pl.BlockSpec(memory_space=pl.ANY)],
        out_specs=(vmem, vmem, vmem),
        scratch_shapes=scratch,
        compiler_params=pltpu.CompilerParams(
            collective_id=0, has_side_effects=True, vmem_limit_bytes=50 * 1024 * 1024
        ),
        cost_estimate=pl.CostEstimate(flops=8_000_000_000, bytes_accessed=8_000_000, transcendentals=0),
    )(
        top_cotangent,
        layer_inputs.reshape(tokens, half),
        router_weight[0].T,
        expert_ids[0].transpose(0, 2, 1).reshape(micro * 2, tok),
        expert_outputs.reshape(tokens, 2, half),
        hidden.reshape(tokens, 2, half_ff),
    )
    return (
        cotangent.reshape(1, micro, tok, half),
        down.reshape(1, 1, 1, tile, half),
        router[:, :strip].T.reshape(1, 1, strip, EXPERTS),
    )


def solution(mesh):
    in_specs = (
        P(None, "ed", "tp"),
        P("section", None, "ed", "tp"),
        P("section", None, None),
        P("section", None, "ed", None),
        P("section", None, "ed", None, "tp"),
        P("section", None, "ed", None, "tp"),
    )
    out_specs = (
        P("section", None, "ed", "tp"),
        P("section", "tp", "ed", None, None),
        P("section", "tp", "ed", None),
    )
    return jax.shard_map(
        per_device, mesh=mesh, in_specs=in_specs, out_specs=out_specs, check_vma=False
    )
```
